32 devices in a mesh: gx: 4 (over z), gy: 8 (over y, x, core).
Axes of the slice: x: 2, y: 2, z: 4, core: 2. Of those that a mesh axis runs over, the one named last changes fastest.
Arguments:
- initial_basis: float32 [8, 64, 128, 128], P(None, 'gx', 'gy'), may hold values from 0.1 to 0.5
- labels: int32 [64, 128, 128], P('gx', 'gy'), may hold values from 0 to 15
- class_perm: float32 [16], replicated, may hold values from 0.01 to 100
- support: int32 [64, 128, 128], P('gx', 'gy'), may hold values from 0 to 255
Outputs:
- basis: float32 [8, 64, 128, 128], P(None, 'gx', 'gy')
- coarse: float32 [27, 4, 8, 8], P(None, 'gx', 'gy')
The draws below stay inside these ranges and needn't reach their ends.
Inputs may be any that keep to these rules, and one draw needn't show every extreme that they name: `support`: bit s of a cell's entry says whether the basis function of its block's corner slot s may be nonzero in that cell.
All inputs are finite; a program needn't handle non-finite values.
Results may differ from the reference program's by a relative error of at most 0.0003.
Values sent between devices are 32-bit elements; how exact they have to be, the bound alone decides.
No kernel may reach another device: no remote copies, remote signals or barrier semaphores. Data moves between devices by JAX's collectives and lax.ppermute only.
A program may use at most 64 MiB of HBM per device.

```python
import math
import jax
import jax.numpy as jnp
import numpy as np
from jax import lax

CB = 16
ITERS = 3
NCLASS = 16
LZ = 128
NX = 64
NY = 128


def set_ends(entries, rng, smallest, largest):
    dims = entries.shape
    place = [jax.random.randint(jax.random.fold_in(rng, axis), (), 0, dims[axis]) for axis in range(len(dims))]
    entries = entries.at[tuple(place)].set(smallest)
    longest = dims.index(max(dims))
    place[longest] = (place[longest] + 1) % dims[longest]
    return entries.at[tuple(place)].set(largest)


def shard_levels(own_key, shape, split, low, largest):
    def one(position, shards_of):
        steps = jax.random.uniform(jax.random.fold_in(jax.random.fold_in(own_key, 6), position), (shards_of,), jnp.float32, low / len(split), largest / len(split))
        return jnp.repeat(jnp.exp(steps), shape[position] // shards_of).reshape((-1,) + (1,) * (len(shape) - position - 1))

    loudness = one(*split[0])
    for cut in split[1:]:
        loudness = loudness * one(*cut)
    return loudness


def rank_table(count, lean):
    weights = [(1 << 20) // math.isqrt(standing ** lean) + 1 for standing in range(1, count + 1)]
    spread = 1 + sum(weights) // (1 << 30)
    return np.cumsum(np.array([max(1, weight // spread) for weight in weights]))


def skewed_ids(own_key, extent, amount, slope):
    listing = rank_table(amount, slope)
    pick = jax.random.randint(jax.random.fold_in(own_key, 1), extent, 0, int(listing[amount - 1]))
    standing = jnp.searchsorted(jnp.asarray(listing, jnp.int32), pick, side="right")
    return jax.random.permutation(jax.random.fold_in(own_key, 2), amount)[standing].astype(jnp.int32)


def setup_inputs(seed: int = 0) -> dict:
    key_of = jax.random.split(jax.random.key(seed), 5)
    return {
        "initial_basis": jnp.clip(0.1 + 0.4 * jax.random.uniform(key_of[0], (8, NX, NY, LZ), jnp.float32) ** shard_levels(key_of[0], (8, NX, NY, LZ), ((1, 4), (2, 8)), -0.2, 0.2), 0.1, 0.5),
        "labels": set_ends(skewed_ids(key_of[1], (NX, NY, LZ), NCLASS, 2), jax.random.fold_in(key_of[1], 3), 0, NCLASS - 1).astype(jnp.int32),
        "class_perm": jnp.clip(jnp.exp(jax.random.uniform(key_of[2], (NCLASS,), jnp.float32, math.log(0.01), math.log(100.0))), 0.01, 100.0),
        "support": set_ends(jax.random.randint(key_of[3], (NX, NY, LZ), 0, 256), jax.random.fold_in(key_of[3], 1), 0, 255).astype(jnp.int32),
    }


omega_jacobi = 2.0 / 3.0
renorm_floor = 0.5


def corner_of(slot_index):
    return ((slot_index >> 2) & 1, (slot_index >> 1) & 1, slot_index & 1)


def slot_remap(values, bit_axis, upward, crossing):
    lower_half = jnp.take(values, 0, axis=bit_axis)
    upper_half = jnp.take(values, 1, axis=bit_axis)
    nothing = jnp.zeros_like(lower_half)
    if upward:
        shifted = jnp.stack([nothing, lower_half], axis=bit_axis)
    else:
        shifted = jnp.stack([upper_half, nothing], axis=bit_axis)
    return jnp.where(crossing, shifted, values)


def conductance(centre, neighbour):
    total_perm = centre + neighbour
    divisor = jnp.where(total_perm > 0.0, total_perm, 1.0)
    return 2.0 * centre * neighbour / divisor


def stencil_terms(basis_pad, perm_pad, x_start, y_start):
    centre = perm_pad[1:-1, 1:-1]
    count_x, count_y, count_z = centre.shape
    basis_core = basis_pad[:, :, :, 1:-1, 1:-1]
    place_x = (jnp.arange(count_x) + x_start) % CB
    place_y = (jnp.arange(count_y) + y_start) % CB
    place_z = jnp.arange(count_z) % CB
    perm_vert = jnp.pad(centre, ((0, 0), (0, 0), (1, 1)))
    basis_vert = jnp.pad(basis_core, ((0, 0), (0, 0), (0, 0), (0, 0), (0, 0), (1, 1)))
    sides = (
        (perm_pad[2:, 1:-1], basis_pad[:, :, :, 2:, 1:-1], 0, True, (place_x == CB - 1)[:, None, None]),
        (perm_pad[:-2, 1:-1], basis_pad[:, :, :, :-2, 1:-1], 0, False, (place_x == 0)[:, None, None]),
        (perm_pad[1:-1, 2:], basis_pad[:, :, :, 1:-1, 2:], 1, True, (place_y == CB - 1)[None, :, None]),
        (perm_pad[1:-1, :-2], basis_pad[:, :, :, 1:-1, :-2], 1, False, (place_y == 0)[None, :, None]),
        (perm_vert[:, :, 2:], basis_vert[:, :, :, :, :, 2:], 2, True, (place_z == CB - 1)[None, None, :]),
        (perm_vert[:, :, :-2], basis_vert[:, :, :, :, :, :-2], 2, False, (place_z == 0)[None, None, :]),
    )
    diagonal = jnp.zeros_like(centre)
    inflow = jnp.zeros_like(basis_core)
    for neighbour, values, bit_axis, upward, crossing in sides:
        linkage = conductance(centre, neighbour)
        diagonal = diagonal + linkage
        inflow = inflow + linkage * slot_remap(values, bit_axis, upward, crossing)
    return basis_core, diagonal, inflow


def jacobi_step(basis_core, diagonal, inflow, valid):
    divisor = jnp.where(diagonal > 0.0, diagonal, 1.0)
    return (basis_core - omega_jacobi * (diagonal * basis_core - inflow) / divisor) * valid


def renormalize(weights):
    totals = jnp.sum(weights, axis=(0, 1, 2))
    return weights / jnp.maximum(totals, renorm_floor)


def support_mask(support, first_x, first_y, limit_x, limit_y, limit_z):
    count_x, count_y, count_z = support.shape
    block_x = (jnp.arange(count_x) + first_x) // CB
    block_y = (jnp.arange(count_y) + first_y) // CB
    block_z = jnp.arange(count_z) // CB
    layers = []
    for slot_index in range(8):
        corner_x, corner_y, corner_z = corner_of(slot_index)
        present = jnp.right_shift(support, slot_index) & 1
        inside = (((block_x + corner_x) < limit_x)[:, None, None]
                  & ((block_y + corner_y) < limit_y)[None, :, None]
                  & ((block_z + corner_z) < limit_z)[None, None, :])
        layers.append(jnp.where(inside & (present > 0), 1.0, 0.0).astype(jnp.float32))
    return jnp.stack(layers).reshape(2, 2, 2, count_x, count_y, count_z)


def block_products(basis_core, image):
    _, _, _, count_x, count_y, count_z = basis_core.shape
    shape_blocks = (8, count_x // CB, CB, count_y // CB, CB, count_z // CB, CB)
    return jnp.einsum("aiujvkw,biujvkw->abijk", basis_core.reshape(shape_blocks),
                      image.reshape(shape_blocks), precision=lax.Precision.HIGHEST)


def assemble(products):
    _, _, count_x, count_y, count_z = products.shape
    assembled = jnp.zeros((27, count_x + 1, count_y + 1, count_z + 1), jnp.float32)
    for first_slot in range(8):
        for second_slot in range(8):
            one_x, one_y, one_z = corner_of(first_slot)
            two_x, two_y, two_z = corner_of(second_slot)
            offset_index = 9 * (two_x - one_x + 1) + 3 * (two_y - one_y + 1) + (two_z - one_z + 1)
            assembled = assembled.at[offset_index, one_x:one_x + count_x, one_y:one_y + count_y,
                                     one_z:one_z + count_z].add(products[first_slot, second_slot])
    return assembled


def reference(initial_basis, labels, class_perm, support):
    count_x, count_y, count_z = labels.shape
    permeability = class_perm[labels]
    valid = support_mask(support, 0, 0, count_x // CB, count_y // CB, count_z // CB)
    weights = initial_basis.reshape(2, 2, 2, count_x, count_y, count_z) * valid
    perm_pad = jnp.pad(permeability, ((1, 1), (1, 1), (0, 0)))
    lateral = ((0, 0), (0, 0), (0, 0), (1, 1), (1, 1), (0, 0))
    for sweep_step in range(ITERS):
        basis_core, diagonal, inflow = stencil_terms(jnp.pad(weights, lateral), perm_pad, 0, 0)
        weights = jacobi_step(basis_core, diagonal, inflow, valid)
    weights = renormalize(weights)
    basis_core, diagonal, inflow = stencil_terms(jnp.pad(weights, lateral), perm_pad, 0, 0)
    image = diagonal * basis_core - inflow
    coarse = assemble(block_products(basis_core, image))[:, :-1, :-1, :-1]
    return weights.reshape(8, count_x, count_y, count_z), coarse
```

```python
import functools

import jax
import jax.numpy as jnp
import numpy as np
from jax import lax
from jax.experimental import pallas as pl
from jax.experimental.pallas import tpu as pltpu
from jax.sharding import PartitionSpec as P

CB = 16
NCLASS = 16
DEPTH = 4
PAD = CB + 2 * DEPTH
SLAB = PAD * PAD
HOME = 8 + 4 * SLAB
ROWS = 16 + 16 * SLAB
LANES = 128
MIB = 1 << 20
F32 = jnp.float32

step_share = 2.0 / 3.0
renorm_floor = 0.5


def in_vmem(shape, dtype=F32):
    return pltpu.VMEM(shape, dtype)


def pinned(array):
    return pltpu.with_memory_space_constraint(array, pltpu.VMEM)


VMEM_SPEC = pl.BlockSpec(memory_space=pltpu.VMEM)
SMEM_SPEC = pl.BlockSpec(memory_space=pltpu.SMEM)
ANY_SPEC = pl.BlockSpec(memory_space=pl.ANY)


def lane_iota():
    return lax.broadcasted_iota(jnp.int32, (8, LANES), 1)


def row_iota():
    return lax.broadcasted_iota(jnp.int32, (8, LANES), 0)


def look_up(label, table):
    level = [table[c] for c in range(NCLASS)]
    for bit in range(4):
        chosen = (label & (1 << bit)) != 0
        level = [jnp.where(chosen, high, low) for low, high in zip(level[0::2], level[1::2])]
    return level[0]


def allowed_bits():
    keep = jnp.int32(255)
    keep = jnp.where(lax.axis_index("gx") == lax.axis_size("gx") - 1, keep & 0x0F, keep)
    keep = jnp.where(lax.axis_index("gy") == lax.axis_size("gy") - 1, keep & 0x33, keep)
    return jnp.where(lane_iota() >= LANES - CB, keep & 0x55, keep)


def is_even(axis):
    return lax.rem(lax.axis_index(axis), 2) == 0


def face_kernel(basis_hbm, labels_hbm, support_hbm, table, out_a, out_b, basis, labels, support, sems):
    copies = []
    for side, start in enumerate((0, CB - DEPTH)):
        here = pl.ds(side * DEPTH, DEPTH)
        there = pl.ds(start, DEPTH)
        copies += [
            pltpu.make_async_copy(labels_hbm.at[there], labels.at[here], sems.at[3 * side]),
            pltpu.make_async_copy(support_hbm.at[there], support.at[here], sems.at[3 * side + 1]),
            pltpu.make_async_copy(basis_hbm.at[:, there], basis.at[:, here], sems.at[3 * side + 2]),
        ]
    for copy in copies:
        copy.start()
    keep = allowed_bits()
    high_first = is_even("gx")
    for copy in copies:
        copy.wait()
    for out, high in ((out_a, high_first), (out_b, jnp.logical_not(high_first))):
        base = jnp.where(high, DEPTH, 0)

        def one_row(x, _, out=out, base=base):
            for tile in (0, 8):
                at = pl.ds(tile, 8)
                bits = support[base + x, at, :] & keep
                for slot in range(8):
                    out[slot, x, at, :] = jnp.where(
                        (bits & (1 << slot)) != 0, basis[slot, base + x, at, :], 0.0
                    )
                out[8, x, at, :] = look_up(labels[base + x, at, :], table)
            return 0

        lax.fori_loop(0, DEPTH, one_row, 0)


def own_kernel(basis, labels, support, table, out):
    keep = allowed_bits()

    def one_row(x, _):
        for tile in (0, 8):
            at = pl.ds(tile, 8)
            bits = support[x, at, :] & keep
            for slot in range(8):
                out[slot, x, at, :] = jnp.where((bits & (1 << slot)) != 0, basis[slot, x, at, :], 0.0)
            out[8, x, at, :] = look_up(labels[x, at, :], table)
        return 0

    lax.fori_loop(0, CB, one_row, 0)


def side_kernel(own, from_a, from_b, out_a, out_b):
    x_even = is_even("gx")
    y_even = is_even("gy")

    def fill(high_out, low_out, high_in, low_in):
        def one_field(s, _):
            for pair in range(PAD // 2 - 1):
                for half in range(2):
                    x = 2 * pair + half - DEPTH + 1
                    if x < 0:
                        source = low_in.at[s, x + DEPTH]
                    elif x < CB:
                        source = own.at[s, x]
                    else:
                        source = high_in.at[s, x - CB]
                    into = pl.ds(half * DEPTH, DEPTH)
                    low_out[s, pair, into, :] = source[0:DEPTH, :]
                    high_out[s, pair, into, :] = source[CB - DEPTH : CB, :]
            return 0

        lax.fori_loop(0, 9, one_field, 0)

    for xe in (True, False):
        for ye in (True, False):

            @pl.when((x_even == xe) & (y_even == ye))
            def _(xe=xe, ye=ye):
                high_out, low_out = (out_a, out_b) if ye else (out_b, out_a)
                high_in, low_in = (from_a, from_b) if xe else (from_b, from_a)
                fill(high_out, low_out, high_in, low_in)


def place(slot, x, y):
    return HOME + (slot * PAD + x) * PAD + y


def main_kernel(own, x_a, x_b, y_a, y_b, group, select, basis_out, rows_out, w_a, w_b, perm, coef, image, acc):
    lane = lane_iota()
    row = row_iota()
    at_last = (lane % CB) == CB - 1
    at_first = (lane % CB) == 0
    zero = jnp.zeros((8, LANES), F32)

    for ref in (w_a, w_b):
        for slot, rows in ((-4, (DEPTH, DEPTH + CB)), (8, (DEPTH - 1, DEPTH + CB - 1))):
            for s in range(slot, slot + 4):
                for x in rows:
                    for tile in range(3):
                        ref[pl.ds(place(s, x, 8 * tile), 8), :] = zero
    for x in (0, PAD - 1):
        for tile in (0, 2):
            perm[pl.ds(8 + x * PAD + 8 * tile, 8), :] = zero
            for s in range(8):
                w_a[pl.ds(place(s, x, 8 * tile), 8), :] = zero
    for ref, end in ((perm, 16 + SLAB), (w_a, ROWS), (w_b, ROWS)):
        ref[0:8, :] = zero
        ref[end - 8 : end, :] = zero

    x_even = is_even("gx")
    y_even = is_even("gy")

    def unpack(s, to, start, high_x, low_x, high_y, low_y):
        for x in range(CB):
            to[pl.ds(start + (x + DEPTH) * PAD + DEPTH, CB), :] = own[s, x]
        for x in range(DEPTH):
            to[pl.ds(start + x * PAD + DEPTH, CB), :] = low_x[s, x]
            to[pl.ds(start + (x + DEPTH + CB) * PAD + DEPTH, CB), :] = high_x[s, x]
        for pair in range(PAD // 2 - 1):
            for half in range(2):
                x = 2 * pair + half + 1
                part = pl.ds(half * DEPTH, DEPTH)
                to[pl.ds(start + x * PAD, DEPTH), :] = low_y[s, pair, part, :]
                to[pl.ds(start + x * PAD + DEPTH + CB, DEPTH), :] = high_y[s, pair, part, :]

    for xe in (True, False):
        for ye in (True, False):

            @pl.when((x_even == xe) & (y_even == ye))
            def _(xe=xe, ye=ye):
                sides = ((x_a, x_b) if xe else (x_b, x_a)) + ((y_a, y_b) if ye else (y_b, y_a))
                unpack(8, perm, 8, *sides)

                def one_slot(s, _):
                    unpack(s, w_a, pl.multiple_of(HOME + s * SLAB, 8), *sides)
                    return 0

                lax.fori_loop(0, 8, one_slot, 0)

    def conductance(one, two):
        return 2.0 * one * two / jnp.maximum(one + two, 1e-30)

    def one_coef(x, before):
        after = []
        for tile in range(3):
            at = pl.multiple_of(8 + x * PAD + 8 * tile, 8)
            here = perm[pl.ds(at, 8), :]
            x_up = conductance(here, perm[pl.ds(at + PAD, 8), :])
            x_down = before[tile]
            after.append(x_up)
            y_up = conductance(here, perm[pl.ds(at + 1, 8), :])
            y_down = conductance(here, perm[pl.ds(at - 1, 8), :])
            z_up = jnp.where(lane == LANES - 1, 0.0, conductance(here, pltpu.roll(here, LANES - 1, 1)))
            z_down = pltpu.roll(z_up, 1, 1)
            diag = ((x_up + x_down) + (y_up + y_down)) + (z_up + z_down)
            scale = step_share / jnp.maximum(diag, 1e-30)
            z_up = z_up * scale
            z_down = z_down * scale
            terms = (
                x_up * scale,
                x_down * scale,
                y_up * scale,
                y_down * scale,
                z_up,
                z_down,
                jnp.where(at_last, 0.0, z_up),
                jnp.where(at_first, 0.0, z_down),
                diag,
            )
            for k, term in enumerate(terms):
                coef[k, pl.ds(at, 8), :] = term
        return tuple(after)

    first = tuple(
        conductance(perm[pl.ds(8 + 8 * tile, 8), :], perm[pl.ds(8 + PAD + 8 * tile, 8), :])
        for tile in range(3)
    )
    lax.fori_loop(1, PAD - 1, one_coef, first)

    def inflow(src, x, y, up_row, down_row, aligned):
        up_slots = jnp.where((x == DEPTH - 1) | (x == DEPTH + CB - 1), PAD - 4 * SLAB, PAD)
        down_slots = jnp.where((x == DEPTH) | (x == DEPTH + CB), 4 * SLAB - PAD, -PAD)
        at = 8 + x * PAD + y
        if aligned:
            at = pl.multiple_of(at, 8)
            up_slots = pl.multiple_of(up_slots, 8)
            down_slots = pl.multiple_of(down_slots, 8)
        k = [coef[i, pl.ds(at, 8), :] for i in range(8)]
        at = at + (HOME - 8)
        centre = [src[pl.ds(at + s * SLAB, 8), :] for s in range(8)]
        total = []
        y_up = [src[pl.ds(at + s * SLAB + 1, 8), :] for s in range(8)]
        y_down = [src[pl.ds(at + s * SLAB - 1, 8), :] for s in range(8)]
        z_up = [pltpu.roll(c, LANES - 1, 1) for c in centre]
        z_down = [pltpu.roll(c, 1, 1) for c in centre]
        for s in range(8):
            got = k[0] * src[pl.ds(at + (s * SLAB) + up_slots, 8), :]
            got = got + k[1] * src[pl.ds(at + (s * SLAB) + down_slots, 8), :]
            value = y_up[s]
            if up_row is not None:
                value = jnp.where(row == up_row, y_up[s ^ 2] if s & 2 else 0.0, value)
            got = got + k[2] * value
            value = y_down[s]
            if down_row is not None:
                value = jnp.where(row == down_row, 0.0 if s & 2 else y_down[s ^ 2], value)
            got = got + k[3] * value
            if s & 1:
                got = got + k[4] * jnp.where(at_last, z_up[s ^ 1], z_up[s])
                got = got + k[7] * z_down[s]
            else:
                got = got + k[6] * z_up[s]
                got = got + k[5] * jnp.where(at_first, z_down[s ^ 1], z_down[s])
            total.append(got)
        return centre, total

    def sweep(src, dst, margin):
        def one_row(x, _):
            for tile in range(3):
                crossing = (None, None) if tile == 1 else (3, 4)
                centre, total = inflow(src, x, 8 * tile, *crossing, True)
                at = pl.multiple_of(HOME + x * PAD + 8 * tile, 8)
                for s in range(8):
                    fresh = centre[s] * (1.0 - step_share) + total[s]
                    dst[pl.ds(at + s * SLAB, 8), :] = jnp.where(centre[s] > 0.0, fresh, 0.0)
            return 0

        lax.fori_loop(margin, PAD - margin, one_row, 0)

    sweep(w_a, w_b, 1)
    sweep(w_b, w_a, 2)
    sweep(w_a, w_b, 3)

    def renormalize(x, _):
        for tile in range(3):
            at = pl.multiple_of(HOME + x * PAD + 8 * tile, 8)
            w = [w_b[pl.ds(at + s * SLAB, 8), :] for s in range(8)]
            total = ((w[0] + w[1]) + (w[2] + w[3])) + ((w[4] + w[5]) + (w[6] + w[7]))
            inverse = 1.0 / jnp.maximum(total, renorm_floor)
            for s in range(8):
                w_a[pl.ds(at + s * SLAB, 8), :] = w[s] * inverse
        return 0

    lax.fori_loop(DEPTH - 1, DEPTH + CB + 1, renormalize, 0)

    def one_image(x, _):
        for tile in (0, 1):
            up_row, down_row = (None, 0) if tile == 0 else (7, None)
            y = DEPTH + 8 * tile
            centre, total = inflow(w_a, x, y, up_row, down_row, False)
            diag = coef[8, pl.ds(8 + x * PAD + y, 8), :]
            for s in range(8):
                basis_out[s, x - DEPTH, pl.ds(8 * tile, 8), :] = centre[s]
                image[s, x - DEPTH, pl.ds(8 * tile, 8), :] = diag * (centre[s] - total[s] * (1.0 / step_share))
        return 0

    lax.fori_loop(DEPTH, DEPTH + CB, one_image, 0)

    for first_slot in (0, 4):

        def one_product(x, sums):
            sums = list(sums)
            for tile in (0, 8):
                at = pl.ds(tile, 8)
                left = [basis_out[first_slot + s, x, at, :] for s in range(4)]
                right = [image[s, x, at, :] for s in range(8)]
                sums = [sums[i] + left[i // 8] * right[i % 8] for i in range(32)]
            return tuple(sums)

        sums = lax.fori_loop(0, CB, one_product, (zero,) * 32)
        for i in range(32):
            acc[8 * first_slot + i] = sums[i]

    reduced = jnp.sum(acc[...], axis=1)
    dot = functools.partial(
        lax.dot_general, precision=lax.Precision.HIGHEST, preferred_element_type=F32
    )
    per_block = dot(group[...], reduced, (((1,), (1,)), ((), ())))
    rows_out[...] = dot(per_block[0:8], select[0:64], (((1,), (0,)), ((), ()))) + dot(
        per_block[8:16], select[64:128], (((1,), (0,)), ((), ()))
    )


def tables():
    blocks = LANES // CB
    group = np.zeros((16, LANES), np.float32)
    for z in range(LANES):
        group[z // CB, z] = 1.0
        if z // CB + 1 < blocks:
            group[8 + z // CB + 1, z] = 1.0
    select = np.zeros((128, LANES), np.float32)
    for one in range(8):
        for two in range(8):
            gap = [((two >> b) & 1) - ((one >> b) & 1) + 1 for b in (2, 1, 0)]
            offset = 9 * gap[0] + 3 * gap[1] + gap[2]
            select[64 * (one & 1) + 8 * one + two, 32 * (one >> 1) + offset] = 1.0
    return group, select


def swap_pairs(axis, first):
    count = lax.axis_size(axis)
    pairs = []
    for a in range(first, count - 1, 2):
        pairs += [(a, a + 1), (a + 1, a)]
    return pairs


def swap_both(first, second, axis):
    return (
        lax.ppermute(first, axis, swap_pairs(axis, 0)),
        lax.ppermute(second, axis, swap_pairs(axis, 1)),
    )


def ahead(array, by_x, by_y):
    count_x, count_y = lax.axis_size("gx"), lax.axis_size("gy")
    pairs = [
        (x * count_y + y, (x + by_x) * count_y + y + by_y)
        for x in range(count_x - by_x)
        for y in range(count_y - by_y)
    ]
    return lax.ppermute(array, ("gx", "gy"), pairs)


def shards(initial_basis, labels, class_perm, support):
    size_x, size_y, size_z = labels.shape
    assert (size_x, size_y, size_z) == (CB, CB, LANES)
    face = (9, DEPTH, CB, LANES)
    face_a, face_b = pl.pallas_call(
        face_kernel,
        out_shape=(in_vmem(face), in_vmem(face)),
        in_specs=[ANY_SPEC, ANY_SPEC, ANY_SPEC, SMEM_SPEC],
        out_specs=(VMEM_SPEC, VMEM_SPEC),
        scratch_shapes=[
            pltpu.VMEM((8, 2 * DEPTH, CB, LANES), F32),
            pltpu.VMEM((2 * DEPTH, CB, LANES), jnp.int32),
            pltpu.VMEM((2 * DEPTH, CB, LANES), jnp.int32),
            pltpu.SemaphoreType.DMA((6,)),
        ],
        compiler_params=pltpu.CompilerParams(vmem_limit_bytes=4 * MIB),
        name="x_faces",
    )(initial_basis, labels, support, class_perm)
    x_a, x_b = swap_both(face_a, face_b, "gx")
    own = pl.pallas_call(
        own_kernel,
        out_shape=in_vmem((9, CB, CB, LANES)),
        in_specs=[VMEM_SPEC, VMEM_SPEC, VMEM_SPEC, SMEM_SPEC],
        out_specs=VMEM_SPEC,
        compiler_params=pltpu.CompilerParams(vmem_limit_bytes=8 * MIB),
        cost_estimate=pl.CostEstimate(flops=1 << 20, bytes_accessed=3 * MIB, transcendentals=0),
        name="own_tile",
    )(initial_basis, labels, support, class_perm)
    side = (9, PAD // 2 - 1, 8, LANES)
    side_a, side_b = pl.pallas_call(
        side_kernel,
        out_shape=(in_vmem(side), in_vmem(side)),
        in_specs=[VMEM_SPEC] * 3,
        out_specs=(VMEM_SPEC, VMEM_SPEC),
        compiler_params=pltpu.CompilerParams(vmem_limit_bytes=8 * MIB),
        name="y_faces",
    )(pinned(own), pinned(x_a), pinned(x_b))
    y_a, y_b = swap_both(side_a, side_b, "gy")
    group, select = tables()
    basis, rows = pl.pallas_call(
        main_kernel,
        out_shape=(jax.ShapeDtypeStruct((8, CB, CB, LANES), F32), in_vmem((8, LANES))),
        in_specs=[VMEM_SPEC] * 7,
        out_specs=(VMEM_SPEC, VMEM_SPEC),
        scratch_shapes=[
            pltpu.VMEM((ROWS, LANES), F32),
            pltpu.VMEM((ROWS, LANES), F32),
            pltpu.VMEM((16 + SLAB, LANES), F32),
            pltpu.VMEM((9, 16 + SLAB, LANES), F32),
            pltpu.VMEM((8, CB, CB, LANES), F32),
            pltpu.VMEM((64, 8, LANES), F32),
        ],
        compiler_params=pltpu.CompilerParams(vmem_limit_bytes=32 * MIB),
        name="sweeps_and_products",
    )(pinned(own), pinned(x_a), pinned(x_b), pinned(y_a), pinned(y_b), jnp.asarray(group), jnp.asarray(select))
    from_x = ahead(rows, 1, 0)
    from_y = ahead(rows, 0, 1)
    from_xy = ahead(rows, 1, 1)
    coarse = (rows[:, 0:27] + from_x[:, 64:91]) + (from_y[:, 32:59] + from_xy[:, 96:123])
    return basis, coarse.T.reshape(27, 1, 1, LANES // CB)


def solution(mesh):
    return jax.shard_map(
        shards,
        mesh=mesh,
        in_specs=(P(None, "gx", "gy", None), P("gx", "gy", None), P(), P("gx", "gy", None)),
        out_specs=(P(None, "gx", "gy", None), P(None, "gx", "gy", None)),
        check_vma=False,
    )
```

```python
import functools

import jax
import jax.numpy as jnp
from jax import lax
from jax.experimental import pallas as pl
from jax.experimental.pallas import tpu as pltpu
from jax.sharding import PartitionSpec as P

CB = 16
NCLASS = 16
DEPTH = 4
PAD = CB + 2 * DEPTH
CELLS = PAD * PAD
LANES = 128
SLOTS = 8
FACE = DEPTH * CB
CORNER = tuple((i, j) for i in range(1, DEPTH) for j in range(1, DEPTH) if i + j <= DEPTH)
MIB = 1 << 20
F32 = jnp.float32

step_share = 2.0 / 3.0
renorm_floor = 0.5

FIELD = (16 + CELLS * SLOTS, LANES)
PLAIN = (16 + CELLS, LANES)
COEF = (7, 16 + CELLS, LANES)
FACE_ROWS = FACE * (SLOTS + 1)
CORNER_ROWS = 112


def in_vmem(*shape):
    return pltpu.VMEM(shape, F32)


def pinned(array):
    return pltpu.with_memory_space_constraint(array, pltpu.VMEM)


def in_hbm(array):
    return pltpu.with_memory_space_constraint(array, pltpu.HBM)


VMEM_SPEC = pl.BlockSpec(memory_space=pltpu.VMEM)
SMEM_SPEC = pl.BlockSpec(memory_space=pltpu.SMEM)
HBM_SPEC = pl.BlockSpec(memory_space=pltpu.HBM)


def lane_iota():
    return lax.broadcasted_iota(jnp.int32, (8, LANES), 1)


def slot_iota():
    return lax.broadcasted_iota(jnp.int32, (8, LANES), 0)


def aligned(row):
    return row if isinstance(row, int) else pl.multiple_of(row, 8)


def column(x, y):
    return 8 + (x + DEPTH) * PAD + y + DEPTH


def field_row(x, y):
    return 8 + ((x + DEPTH) * PAD + y + DEPTH) * SLOTS


def is_even(axis):
    return lax.rem(lax.axis_index(axis), 2) == 0


def look_up(label, table):
    level = [table[c] for c in range(NCLASS)]
    for bit in range(4):
        chosen = (label & (1 << bit)) != 0
        level = [jnp.where(chosen, high, low) for low, high in zip(level[0::2], level[1::2])]
    return level[0]


def slot_bits():
    keep = jnp.int32(255)
    keep = jnp.where(lax.axis_index("gx") == lax.axis_size("gx") - 1, keep & 0x0F, keep)
    keep = jnp.where(lax.axis_index("gy") == lax.axis_size("gy") - 1, keep & 0x33, keep)
    keep = jnp.where(lane_iota() >= LANES - CB, keep & 0x55, keep)
    return keep & (1 << slot_iota())


def first_weights(basis, start, stride, support_row, bits):
    found = jnp.broadcast_to(support_row, (8, LANES)) & bits
    return jnp.where(found != 0, basis[pl.ds(start, SLOTS, stride=stride), :], 0.0)


def x_face_kernel(basis_hbm, labels_hbm, support_hbm, table, out_a, out_b, basis, labels, support, sems):
    copies = []
    for side, start in enumerate((0, CB - DEPTH)):
        there = pl.ds(start, DEPTH)
        copies += [
            pltpu.make_async_copy(basis_hbm.at[:, there], basis.at[side], sems.at[3 * side]),
            pltpu.make_async_copy(labels_hbm.at[there], labels.at[side], sems.at[3 * side + 1]),
            pltpu.make_async_copy(support_hbm.at[there], support.at[side], sems.at[3 * side + 2]),
        ]
    for copy in copies:
        copy.start()
    bits = slot_bits()
    high_first = is_even("gx")
    for copy in copies:
        copy.wait()
    basis = basis.reshape(2 * SLOTS * FACE, LANES)
    labels = labels.reshape(2 * FACE, LANES)
    support = support.reshape(2 * FACE, LANES)
    for out, high in ((out_a, high_first), (out_b, jnp.logical_not(high_first))):
        side = jnp.where(high, 1, 0)
        for tile in range(0, FACE, 8):
            at = pl.ds(pl.multiple_of(side * FACE + tile, 8), 8)
            out[SLOTS * FACE + tile : SLOTS * FACE + tile + 8, :] = look_up(labels[at, :], table)

        def one_x(x, _, out=out, side=side):
            for y in range(CB):
                cell = x * CB + y
                out[pl.ds(pl.multiple_of(cell * SLOTS, 8), SLOTS), :] = first_weights(
                    basis, side * (SLOTS * FACE) + cell, FACE, support[pl.ds(side * FACE + cell, 1), :], bits
                )
            return 0

        lax.fori_loop(0, DEPTH, one_x, 0)


def own_kernel(basis_hbm, labels_hbm, support_hbm, table, field, perm, out_a, out_b, basis, labels, support, sems):
    copies = [
        pltpu.make_async_copy(basis_hbm, basis, sems.at[0]),
        pltpu.make_async_copy(labels_hbm, labels, sems.at[1]),
        pltpu.make_async_copy(support_hbm, support, sems.at[2]),
    ]
    for copy in copies:
        copy.start()
    bits = slot_bits()
    for copy in copies:
        copy.wait()
    basis = basis.reshape(SLOTS * CB * CB, LANES)
    support = support.reshape(CB * CB, LANES)

    def one_x(x, _):
        for tile in (0, 8):
            perm[pl.ds(column(x, tile), 8), :] = look_up(labels[x, tile : tile + 8, :], table)
        for y in range(CB):
            field[pl.ds(aligned(field_row(x, y)), SLOTS), :] = first_weights(
                basis, x * CB + y, CB * CB, support[pl.ds(x * CB + y, 1), :], bits
            )
        return 0

    lax.fori_loop(0, CB, one_x, 0)

    even = is_even("gy")
    for out, high in ((out_a, even), (out_b, jnp.logical_not(even))):
        start = jnp.where(high, CB - DEPTH, 0)

        def one_face_x(x, _, out=out, start=start):
            out[pl.ds(SLOTS * FACE + x * DEPTH, DEPTH), :] = perm[pl.ds(column(x, start), DEPTH), :]
            for y in range(DEPTH):
                into = pl.multiple_of((x * DEPTH + y) * SLOTS, 8)
                out[pl.ds(into, SLOTS), :] = field[pl.ds(aligned(field_row(x, start + y)), SLOTS), :]
            return 0

        lax.fori_loop(0, CB, one_face_x, 0)


def corner_kernel(from_a, from_b, out_a, out_b):
    x_even = is_even("gx")
    y_even = is_even("gy")
    for even in (True, False):

        @pl.when(x_even == even)
        def _(even=even):
            high_x, low_x = (from_a, from_b) if even else (from_b, from_a)
            for out, high in ((out_a, y_even), (out_b, jnp.logical_not(y_even))):
                n = 0
                for source, row in ((low_x, lambda i: DEPTH - i), (high_x, lambda i: i - 1)):
                    for i, j in CORNER:
                        cell = row(i) * CB + jnp.where(high, CB - j, j - 1)
                        out[SLOTS * n : SLOTS * n + SLOTS, :] = source[
                            pl.ds(pl.multiple_of(cell * SLOTS, 8), SLOTS), :
                        ]
                        at = SLOTS * 2 * len(CORNER) + n
                        out[at : at + 1, :] = source[pl.ds(SLOTS * FACE + cell, 1), :]
                        n += 1


def conductance(one, two):
    return 2.0 * one * two / jnp.maximum(one + two, 1e-30)


def fill_coef(perm, coef, xs):
    lane = lane_iota()
    for x in xs:
        for tile in range(3):
            at = aligned(column(x, 8 * tile - DEPTH))
            here = perm[pl.ds(at, 8), :]
            x_up = conductance(here, perm[pl.ds(at + PAD, 8), :])
            x_down = conductance(here, perm[pl.ds(at - PAD, 8), :])
            y_up = conductance(here, perm[pl.ds(at + 1, 8), :])
            y_down = conductance(here, perm[pl.ds(at - 1, 8), :])
            z_up = jnp.where(lane == LANES - 1, 0.0, conductance(here, pltpu.roll(here, LANES - 1, 1)))
            z_down = jnp.where(lane == 0, 0.0, conductance(here, pltpu.roll(here, 1, 1)))
            diag = ((x_up + x_down) + (y_up + y_down)) + (z_up + z_down)
            scale = step_share / jnp.maximum(diag, 1e-30)
            for k, term in enumerate((x_up, x_down, y_up, y_down, z_up, z_down)):
                coef[k, pl.ds(at, 8), :] = term * scale
            coef[6, pl.ds(at, 8), :] = diag


class Stencil:
    def __init__(self, coef):
        self.coef = coef
        slot = slot_iota()
        lane = lane_iota()
        self.x_bit = slot >= 4
        self.y_bit = (slot & 2) != 0
        self.z_bit = (slot & 1) != 0
        self.first = (lane % CB) == 0
        self.last = (lane % CB) == CB - 1

    def turned(self, src, cells):
        out = []
        for x, y in cells:
            at = aligned(field_row(x, y))
            here = src[pl.ds(at, SLOTS), :]
            above = jnp.where(self.z_bit, src[pl.ds(at - 1, SLOTS), :], 0.0)
            below = jnp.where(self.z_bit, 0.0, src[pl.ds(at + 1, SLOTS), :])
            out.append(pltpu.roll(jnp.where(self.first, above, here), LANES - 1, 1))
            out.append(pltpu.roll(jnp.where(self.last, below, here), 1, 1))
        return tuple(out)

    def lateral(self, src, x, y):
        at = aligned(field_row(x, y))
        step = PAD * SLOTS

        def read(offset):
            return src[pl.ds(at + offset, SLOTS), :]

        def crosses(place, where):
            return isinstance(place, int) and place in where

        up, down = (-1, CB - 1), (0, CB)
        x_up = jnp.where(self.x_bit, read(step - 4), 0.0) if crosses(x, up) else read(step)
        x_down = jnp.where(self.x_bit, 0.0, read(4 - step)) if crosses(x, down) else read(-step)
        y_up = jnp.where(self.y_bit, read(SLOTS - 2), 0.0) if crosses(y, up) else read(SLOTS)
        y_down = jnp.where(self.y_bit, 0.0, read(2 - SLOTS)) if crosses(y, down) else read(-SLOTS)
        return x_up, x_down, y_up, y_down

    def inflow(self, src, x, y, z_up, z_down):
        at = column(x, y)
        total = None
        for k, value in enumerate((*self.lateral(src, x, y), z_up, z_down)):
            term = jnp.broadcast_to(self.coef[k, pl.ds(at, 1), :], (8, LANES)) * value
            total = term if total is None else total + term
        return total

    def sweep(self, src, dst, cells, turned, last):
        for n, (x, y) in enumerate(cells):
            at = aligned(field_row(x, y))
            here = src[pl.ds(at, SLOTS), :]
            fresh = here * (1.0 - step_share) + self.inflow(src, x, y, turned[2 * n], turned[2 * n + 1])
            fresh = jnp.where(here > 0.0, fresh, 0.0)
            if last:
                total = fresh + pltpu.roll(fresh, 4, 0)
                total = total + pltpu.roll(total, 2, 0)
                total = total + pltpu.roll(total, 1, 0)
                fresh = fresh * (1.0 / jnp.maximum(total, renorm_floor))
            dst[pl.ds(at, SLOTS), :] = fresh

    def product(self, src, cells, turned, sums):
        sums = list(sums)
        for n, (x, y) in enumerate(cells):
            at = aligned(field_row(x, y))
            here = src[pl.ds(at, SLOTS), :]
            inflow = self.inflow(src, x, y, turned[2 * n], turned[2 * n + 1])
            diag = jnp.broadcast_to(self.coef[6, pl.ds(column(x, y), 1), :], (8, LANES))
            image = diag * (here - inflow * (1.0 / step_share))
            for s in range(SLOTS):
                sums[s] = sums[s] + jnp.broadcast_to(src[pl.ds(at + s, 1), :], (8, LANES)) * image
        return tuple(sums)


def run_stage(coef, field_a, field_b, sums, cells_at, steps_of):
    stencil = Stencil(coef)
    fields = (field_a, field_b)
    for level in (1, 2, 3, 4):
        src, dst = fields[(level - 1) % 2], fields[level % 2]
        if level == 4:
            src = field_b
        steps = steps_of(level)
        if steps is None:
            cells = cells_at(level, None)
            turned = stencil.turned(src, cells)
            if level < 4:
                stencil.sweep(src, dst, cells, turned, level == 3)
            else:
                sums = stencil.product(src, cells, turned, sums)
            continue
        start, stop, stride = steps
        first = stencil.turned(src, cells_at(level, start))
        if level < 4:

            def body(n, turned, level=level, src=src, dst=dst, start=start, stride=stride):
                i = start + n * stride
                after = stencil.turned(src, cells_at(level, i + stride))
                stencil.sweep(src, dst, cells_at(level, i), turned, level == 3)
                return after

            lax.fori_loop(0, (stop - start) // stride, body, first)
        else:

            def body(n, carry, level=level, src=src, start=start, stride=stride):
                turned, so_far = carry
                i = start + n * stride
                after = stencil.turned(src, cells_at(level, i + stride))
                return after, stencil.product(src, cells_at(level, i), turned, so_far)

            _, sums = lax.fori_loop(0, (stop - start) // stride, body, (first, sums))
    return sums


def inner_kernel(field_in, perm, field_a, field_b, coef, acc):
    del field_in

    def some_coef(n, _):
        fill_coef(perm, coef, (1 + 2 * n, 2 + 2 * n))
        return 0

    lax.fori_loop(0, (CB - 2) // 2, some_coef, 0)

    def cells_at(level, i):
        return [(i + u, y) for u in range(2) for y in range(level, CB - level)]

    zero = jnp.zeros((8, LANES), F32)
    sums = run_stage(
        coef, field_a, field_b, (zero,) * SLOTS, cells_at, lambda level: (level, CB - level, 2)
    )
    for s in range(SLOTS):
        acc[8 * s : 8 * s + 8, :] = sums[s]


def strip_kernel(*refs):
    x_a, x_b, y_a, y_b = refs[:4]
    perm, field_a, field_b, coef, acc = refs[9:]

    for even in (True, False):

        @pl.when(is_even("gx") == even)
        def _(even=even):
            high, low = (x_a, x_b) if even else (x_b, x_a)
            for source, start in ((low, -DEPTH), (high, CB)):

                def one_x(x, _, source=source, start=start):
                    for y in range(CB):
                        at = pl.multiple_of((x * CB + y) * SLOTS, 8)
                        field_a[pl.ds(aligned(field_row(start + x, y)), SLOTS), :] = source[pl.ds(at, SLOTS), :]
                    at = pl.multiple_of(SLOTS * FACE + x * CB, 8)
                    perm[pl.ds(column(start + x, 0), CB), :] = source[pl.ds(at, CB), :]
                    return 0

                lax.fori_loop(0, DEPTH, one_x, 0)

        @pl.when(is_even("gy") == even)
        def _(even=even):
            high, low = (y_a, y_b) if even else (y_b, y_a)

            def one_x(x, _):
                for source, start in ((low, -DEPTH), (high, CB)):
                    for y in range(DEPTH):
                        at = pl.multiple_of((x * DEPTH + y) * SLOTS, 8)
                        field_a[pl.ds(aligned(field_row(x, start + y)), SLOTS), :] = source[pl.ds(at, SLOTS), :]
                    perm[pl.ds(column(x, start), DEPTH), :] = source[pl.ds(SLOTS * FACE + x * DEPTH, DEPTH), :]
                return 0

            lax.fori_loop(0, CB, one_x, 0)

    def some_coef(n, _):
        fill_coef(perm, coef, (2 * n + 1 - DEPTH, 2 * n + 2 - DEPTH))
        return 0

    lax.fori_loop(0, (PAD - 2) // 2, some_coef, 0)

    def cells_at(level, i):
        across = list(range(level - DEPTH, level)) + list(range(CB - level, CB - level + DEPTH))
        return [(x, i) for x in across] + [(i, y) for y in across]

    sums = tuple(acc[8 * s : 8 * s + 8, :] for s in range(SLOTS))
    sums = run_stage(coef, field_a, field_b, sums, cells_at, lambda level: (level, CB - level, 1))
    for s in range(SLOTS):
        acc[8 * s : 8 * s + 8, :] = sums[s]


def node_tables():
    node = lax.broadcasted_iota(jnp.int32, (16, LANES), 0)
    lane = lax.broadcasted_iota(jnp.int32, (16, LANES), 1)
    block = lane // CB
    group = jnp.where((node == block) | (node == block + 9), 1.0, 0.0)
    pair = lax.broadcasted_iota(jnp.int32, (128, LANES), 0)
    lane = lax.broadcasted_iota(jnp.int32, (128, LANES), 1)
    one, two = (pair >> 3) & 7, pair & 7
    offset = 13
    for bit, weight in ((2, 9), (1, 3), (0, 1)):
        offset = offset + weight * (((two >> bit) & 1) - ((one >> bit) & 1))
    goes = (lane == 32 * (one >> 1) + offset) & ((one & 1) == (pair >> 6))
    return group, jnp.where(goes, 1.0, 0.0)


def corner_cells(level):
    cells = []
    for x in list(range(level - DEPTH, level)) + list(range(CB - level, CB - level + DEPTH)):
        for y in list(range(level - DEPTH, level)) + list(range(CB - level, CB - level + DEPTH)):
            out_x = max(-x, x - CB + 1, 0)
            out_y = max(-y, y - CB + 1, 0)
            if out_x + out_y <= DEPTH - level:
                cells.append((x, y))
    return cells


def last_kernel(*refs):
    c_a, c_b = refs[:2]
    rows_out, perm, field_a, field_b, coef = refs[7:12]
    acc = refs[6]

    for even in (True, False):

        @pl.when(is_even("gy") == even)
        def _(even=even):
            high, low = (c_a, c_b) if even else (c_b, c_a)
            for source, y_of in ((low, lambda j: -j), (high, lambda j: CB - 1 + j)):
                n = 0
                for x_of in (lambda i: -i, lambda i: CB - 1 + i):
                    for i, j in CORNER:
                        x, y = x_of(i), y_of(j)
                        at = field_row(x, y)
                        field_a[at : at + SLOTS, :] = source[SLOTS * n : SLOTS * n + SLOTS, :]
                        at = SLOTS * 2 * len(CORNER) + n
                        perm[column(x, y) : column(x, y) + 1, :] = source[at : at + 1, :]
                        n += 1

    for x in (-3, -1, CB - 1, CB + 1):
        fill_coef(perm, coef, (x, x + 1))

    sums = tuple(acc[8 * s : 8 * s + 8, :] for s in range(SLOTS))
    sums = run_stage(
        coef, field_a, field_b, sums, lambda level, i: corner_cells(level), lambda level: None
    )
    group, select = node_tables()
    reduced = jnp.concatenate(sums, axis=0)
    dot = functools.partial(
        lax.dot_general, precision=lax.Precision.HIGHEST, preferred_element_type=F32
    )
    per_block = dot(group, reduced, (((1,), (1,)), ((), ())))
    rows_out[...] = dot(per_block[0:8], select[0:64], (((1,), (0,)), ((), ()))) + dot(
        per_block[8:16], select[64:128], (((1,), (0,)), ((), ()))
    )


def basis_kernel(field, out):
    flat = out.reshape(SLOTS * CB * CB, LANES)

    def one_x(x, _):
        for y in range(CB):
            flat[pl.ds(x * CB + y, SLOTS, stride=CB * CB), :] = field[pl.ds(aligned(field_row(x, y)), SLOTS), :]
        return 0

    lax.fori_loop(0, CB, one_x, 0)


def swap_pairs(axis, first):
    count = lax.axis_size(axis)
    pairs = []
    for a in range(first, count - 1, 2):
        pairs += [(a, a + 1), (a + 1, a)]
    return pairs


def swap_both(first, second, axis):
    return (
        lax.ppermute(first, axis, swap_pairs(axis, 0)),
        lax.ppermute(second, axis, swap_pairs(axis, 1)),
    )


def ahead(array, by_x, by_y):
    count_x, count_y = lax.axis_size("gx"), lax.axis_size("gy")
    pairs = [
        (x * count_y + y, (x + by_x) * count_y + y + by_y)
        for x in range(count_x - by_x)
        for y in range(count_y - by_y)
    ]
    return lax.ppermute(array, ("gx", "gy"), pairs)


def params(mib):
    return pltpu.CompilerParams(vmem_limit_bytes=mib * MIB)


def shards(initial_basis, labels, class_perm, support):
    size_x, size_y, size_z = labels.shape
    assert (size_x, size_y, size_z) == (CB, CB, LANES)
    whole = [in_hbm(initial_basis), in_hbm(labels), in_hbm(support)]
    face = in_vmem(FACE_ROWS, LANES)
    x_face_a, x_face_b = pl.pallas_call(
        x_face_kernel,
        out_shape=(face, face),
        in_specs=[HBM_SPEC] * 3 + [SMEM_SPEC],
        out_specs=(VMEM_SPEC,) * 2,
        scratch_shapes=[
            pltpu.VMEM((2, SLOTS, DEPTH, CB, LANES), F32),
            pltpu.VMEM((2, DEPTH, CB, LANES), jnp.int32),
            pltpu.VMEM((2, DEPTH, CB, LANES), jnp.int32),
            pltpu.SemaphoreType.DMA((6,)),
        ],
        compiler_params=params(4),
        name="x_faces",
    )(*whole, class_perm)
    x_a, x_b = swap_both(x_face_a, x_face_b, "gx")
    field, perm, y_face_a, y_face_b = pl.pallas_call(
        own_kernel,
        out_shape=(in_vmem(*FIELD), in_vmem(*PLAIN), face, face),
        in_specs=[HBM_SPEC] * 3 + [SMEM_SPEC],
        out_specs=(VMEM_SPEC,) * 4,
        scratch_shapes=[
            pltpu.VMEM((SLOTS, CB, CB, LANES), F32),
            pltpu.VMEM((CB, CB, LANES), jnp.int32),
            pltpu.VMEM((CB, CB, LANES), jnp.int32),
            pltpu.SemaphoreType.DMA((3,)),
        ],
        compiler_params=params(4),
        name="own_tile",
    )(*whole, class_perm)
    y_a, y_b = swap_both(y_face_a, y_face_b, "gy")
    field_a, field_b, coef, acc = pl.pallas_call(
        inner_kernel,
        out_shape=(in_vmem(*FIELD), in_vmem(*FIELD), in_vmem(*COEF), in_vmem(64, LANES)),
        in_specs=[VMEM_SPEC] * 2,
        out_specs=(VMEM_SPEC,) * 4,
        input_output_aliases={0: 0},
        compiler_params=params(4),
        cost_estimate=pl.CostEstimate(flops=10 * MIB, bytes_accessed=8 * MIB, transcendentals=0),
        name="inner_stage",
    )(pinned(field), pinned(perm))
    corner = in_vmem(CORNER_ROWS, LANES)
    corner_a, corner_b = pl.pallas_call(
        corner_kernel,
        out_shape=(corner, corner),
        in_specs=[VMEM_SPEC] * 2,
        out_specs=(VMEM_SPEC,) * 2,
        compiler_params=params(4),
        name="corners",
    )(pinned(x_a), pinned(x_b))
    c_a, c_b = swap_both(corner_a, corner_b, "gy")
    perm, field_a, field_b, coef, acc = pl.pallas_call(
        strip_kernel,
        out_shape=(in_vmem(*PLAIN), in_vmem(*FIELD), in_vmem(*FIELD), in_vmem(*COEF), in_vmem(64, LANES)),
        in_specs=[VMEM_SPEC] * 9,
        out_specs=(VMEM_SPEC,) * 5,
        input_output_aliases={4: 0, 5: 1, 6: 2, 7: 3, 8: 4},
        compiler_params=params(4),
        cost_estimate=pl.CostEstimate(flops=10 * MIB, bytes_accessed=8 * MIB, transcendentals=0),
        name="strip_stage",
    )(*[pinned(a) for a in (x_a, x_b, y_a, y_b, perm, field_a, field_b, coef, acc)])
    rows, _, _, field_b, _ = pl.pallas_call(
        last_kernel,
        out_shape=(in_vmem(8, LANES), in_vmem(*PLAIN), in_vmem(*FIELD), in_vmem(*FIELD), in_vmem(*COEF)),
        in_specs=[VMEM_SPEC] * 7,
        out_specs=(VMEM_SPEC,) * 5,
        input_output_aliases={2: 1, 3: 2, 4: 3, 5: 4},
        compiler_params=params(4),
        name="corner_stage",
    )(*[pinned(a) for a in (c_a, c_b, perm, field_a, field_b, coef, acc)])
    from_x = ahead(rows, 1, 0)
    from_y = ahead(rows, 0, 1)
    from_xy = ahead(rows, 1, 1)
    basis = pl.pallas_call(
        basis_kernel,
        out_shape=jax.ShapeDtypeStruct((SLOTS, CB, CB, LANES), F32),
        in_specs=[VMEM_SPEC],
        out_specs=VMEM_SPEC,
        compiler_params=params(4),
        cost_estimate=pl.CostEstimate(flops=0, bytes_accessed=2 * MIB, transcendentals=0),
        name="basis_out",
    )(pinned(field_b))
    coarse = (rows[:, 0:27] + from_x[:, 64:91]) + (from_y[:, 32:59] + from_xy[:, 96:123])
    return basis, coarse.T.reshape(27, 1, 1, LANES // CB)


def solution(mesh):
    return jax.shard_map(
        shards,
        mesh=mesh,
        in_specs=(P(None, "gx", "gy", None), P("gx", "gy", None), P(), P("gx", "gy", None)),
        out_specs=(P(None, "gx", "gy", None), P(None, "gx", "gy", None)),
        check_vma=False,
    )
```

```python
import functools

import jax
import jax.numpy as jnp
from jax import lax
from jax.experimental import pallas as pl
from jax.experimental.pallas import tpu as pltpu
from jax.sharding import PartitionSpec as P

CB = 16
NCLASS = 16
DEPTH = 4
PAD = CB + 2 * DEPTH
CELLS = PAD * PAD
LANES = 128
SLOTS = 8
FACE = DEPTH * CB
CORNER = tuple((i, j) for i in range(1, DEPTH) for j in range(1, DEPTH) if i + j <= DEPTH)
MIB = 1 << 20
F32 = jnp.float32

step_share = 2.0 / 3.0
renorm_floor = 0.5

FIELD = (16 + CELLS * SLOTS, LANES)
PLAIN = (16 + CELLS, LANES)
COEF = (7, 16 + CELLS, LANES)
FACE_ROWS = FACE * (SLOTS + 1)
CORNER_ROWS = 112


def in_vmem(*shape):
    return pltpu.VMEM(shape, F32)


def pinned(array):
    return pltpu.with_memory_space_constraint(array, pltpu.VMEM)


def in_hbm(array):
    return pltpu.with_memory_space_constraint(array, pltpu.HBM)


VMEM_SPEC = pl.BlockSpec(memory_space=pltpu.VMEM)
SMEM_SPEC = pl.BlockSpec(memory_space=pltpu.SMEM)
HBM_SPEC = pl.BlockSpec(memory_space=pltpu.HBM)


def lane_iota():
    return lax.broadcasted_iota(jnp.int32, (8, LANES), 1)


def slot_iota():
    return lax.broadcasted_iota(jnp.int32, (8, LANES), 0)


def aligned(row):
    return row if isinstance(row, int) else pl.multiple_of(row, 8)


def column(x, y):
    return 8 + (x + DEPTH) * PAD + y + DEPTH


def field_row(x, y):
    return 8 + ((x + DEPTH) * PAD + y + DEPTH) * SLOTS


def is_even(axis):
    return lax.rem(lax.axis_index(axis), 2) == 0


def look_up(label, table):
    level = [table[c] for c in range(NCLASS)]
    for bit in range(4):
        chosen = (label & (1 << bit)) != 0
        level = [jnp.where(chosen, high, low) for low, high in zip(level[0::2], level[1::2])]
    return level[0]


def slot_bits():
    keep = jnp.int32(255)
    keep = jnp.where(lax.axis_index("gx") == lax.axis_size("gx") - 1, keep & 0x0F, keep)
    keep = jnp.where(lax.axis_index("gy") == lax.axis_size("gy") - 1, keep & 0x33, keep)
    keep = jnp.where(lane_iota() >= LANES - CB, keep & 0x55, keep)
    return keep & (1 << slot_iota())


def first_weights(basis, start, stride, support_row, bits):
    found = jnp.broadcast_to(support_row, (8, LANES)) & bits
    return jnp.where(found != 0, basis[pl.ds(start, SLOTS, stride=stride), :], 0.0)


def own_kernel(
    basis_hbm, labels_hbm, support_hbm, table_hbm, field, perm, x_a, x_b, y_a, y_b, basis, labels, support, table, sems
):
    fetch_table = pltpu.make_async_copy(table_hbm, table, sems.at[0])
    fetch_labels = pltpu.make_async_copy(labels_hbm, labels, sems.at[1])
    fetch_support = pltpu.make_async_copy(support_hbm, support, sems.at[2])
    fetch_basis = [
        pltpu.make_async_copy(basis_hbm.at[:, pl.ds(DEPTH * part, DEPTH)], basis.at[part], sems.at[3 + part])
        for part in range(CB // DEPTH)
    ]
    for copy in (fetch_table, fetch_labels, fetch_support, *fetch_basis):
        copy.start()
    bits = slot_bits()
    fetch_table.wait()
    fetch_labels.wait()

    def one_perm(x, _):
        for tile in (0, 8):
            perm[pl.ds(column(x, tile), 8), :] = look_up(labels[x, tile : tile + 8, :], table)
        return 0

    lax.fori_loop(0, CB, one_perm, 0, unroll=4)
    fetch_support.wait()
    for copy in fetch_basis:
        copy.wait()
    basis = basis.reshape(SLOTS * CB * CB, LANES)
    support = support.reshape(CB * CB, LANES)

    def one_x(x, _):
        for y in range(CB):
            start = (x // DEPTH) * (SLOTS * FACE) + (x % DEPTH) * CB + y
            field[pl.ds(aligned(field_row(x, y)), SLOTS), :] = first_weights(
                basis, start, FACE, support[pl.ds(x * CB + y, 1), :], bits
            )
        return 0

    lax.fori_loop(0, CB, one_x, 0, unroll=2)

    def x_face(out, start):
        out[SLOTS * FACE : FACE_ROWS, :] = jnp.concatenate(
            [perm[column(start + x, 0) : column(start + x, 0) + CB, :] for x in range(DEPTH)], axis=0
        )
        for x in range(DEPTH):
            rows = CB * SLOTS
            out[x * rows : (x + 1) * rows, :] = field[field_row(start + x, 0) : field_row(start + x, CB), :]

    def y_face(out, start):
        rows = DEPTH * SLOTS
        for x in range(CB):
            at = SLOTS * FACE + x * DEPTH
            out[at : at + DEPTH, :] = perm[column(x, start) : column(x, start + DEPTH), :]
            out[x * rows : (x + 1) * rows, :] = field[field_row(x, start) : field_row(x, start + DEPTH), :]

    for even in (True, False):

        @pl.when(is_even("gx") == even)
        def _(even=even):
            high, low = (x_a, x_b) if even else (x_b, x_a)
            x_face(low, 0)
            x_face(high, CB - DEPTH)

        @pl.when(is_even("gy") == even)
        def _(even=even):
            high, low = (y_a, y_b) if even else (y_b, y_a)
            y_face(low, 0)
            y_face(high, CB - DEPTH)


def corner_kernel(from_a, from_b, inner_done, out_a, out_b):
    del inner_done
    x_even = is_even("gx")
    y_even = is_even("gy")
    for even in (True, False):

        @pl.when(x_even == even)
        def _(even=even):
            high_x, low_x = (from_a, from_b) if even else (from_b, from_a)
            for out, high in ((out_a, y_even), (out_b, jnp.logical_not(y_even))):
                n = 0
                for source, row in ((low_x, lambda i: DEPTH - i), (high_x, lambda i: i - 1)):
                    for i, j in CORNER:
                        cell = row(i) * CB + jnp.where(high, CB - j, j - 1)
                        out[SLOTS * n : SLOTS * n + SLOTS, :] = source[
                            pl.ds(pl.multiple_of(cell * SLOTS, 8), SLOTS), :
                        ]
                        at = SLOTS * 2 * len(CORNER) + n
                        out[at : at + 1, :] = source[pl.ds(SLOTS * FACE + cell, 1), :]
                        n += 1


def conductance(one, two):
    return 2.0 * one * two / jnp.maximum(one + two, 1e-30)


def fill_coef(perm, coef, xs):
    lane = lane_iota()
    for x in xs:
        for tile in range(3):
            at = aligned(column(x, 8 * tile - DEPTH))
            here = perm[pl.ds(at, 8), :]
            x_up = conductance(here, perm[pl.ds(at + PAD, 8), :])
            x_down = conductance(here, perm[pl.ds(at - PAD, 8), :])
            y_up = conductance(here, perm[pl.ds(at + 1, 8), :])
            y_down = conductance(here, perm[pl.ds(at - 1, 8), :])
            z_up = jnp.where(lane == LANES - 1, 0.0, conductance(here, pltpu.roll(here, LANES - 1, 1)))
            z_down = jnp.where(lane == 0, 0.0, conductance(here, pltpu.roll(here, 1, 1)))
            diag = ((x_up + x_down) + (y_up + y_down)) + (z_up + z_down)
            scale = step_share / jnp.maximum(diag, 1e-30)
            for k, term in enumerate((x_up, x_down, y_up, y_down, z_up, z_down)):
                coef[k, pl.ds(at, 8), :] = term * scale
            coef[6, pl.ds(at, 8), :] = diag


class Stencil:
    def __init__(self, coef):
        self.coef = coef
        slot = slot_iota()
        lane = lane_iota()
        self.x_bit = slot >= 4
        self.y_bit = (slot & 2) != 0
        self.z_bit = (slot & 1) != 0
        self.first = (lane % CB) == 0
        self.last = (lane % CB) == CB - 1

    def turned(self, src, cells):
        out = []
        for x, y in cells:
            at = aligned(field_row(x, y))
            here = src[pl.ds(at, SLOTS), :]
            above = jnp.where(self.z_bit, src[pl.ds(at - 1, SLOTS), :], 0.0)
            below = jnp.where(self.z_bit, 0.0, src[pl.ds(at + 1, SLOTS), :])
            out.append(pltpu.roll(jnp.where(self.first, above, here), LANES - 1, 1))
            out.append(pltpu.roll(jnp.where(self.last, below, here), 1, 1))
        return tuple(out)

    def lateral(self, src, x, y):
        at = aligned(field_row(x, y))
        step = PAD * SLOTS

        def read(offset):
            return src[pl.ds(at + offset, SLOTS), :]

        def crosses(place, where):
            return isinstance(place, int) and place in where

        up, down = (-1, CB - 1), (0, CB)
        x_up = jnp.where(self.x_bit, read(step - 4), 0.0) if crosses(x, up) else read(step)
        x_down = jnp.where(self.x_bit, 0.0, read(4 - step)) if crosses(x, down) else read(-step)
        y_up = jnp.where(self.y_bit, read(SLOTS - 2), 0.0) if crosses(y, up) else read(SLOTS)
        y_down = jnp.where(self.y_bit, 0.0, read(2 - SLOTS)) if crosses(y, down) else read(-SLOTS)
        return x_up, x_down, y_up, y_down

    def inflow(self, src, x, y, z_up, z_down):
        at = column(x, y)
        total = None
        for k, value in enumerate((*self.lateral(src, x, y), z_up, z_down)):
            term = jnp.broadcast_to(self.coef[k, pl.ds(at, 1), :], (8, LANES)) * value
            total = term if total is None else total + term
        return total

    def sweep(self, src, dst, cells, turned, last):
        for n, (x, y) in enumerate(cells):
            at = aligned(field_row(x, y))
            here = src[pl.ds(at, SLOTS), :]
            fresh = here * (1.0 - step_share) + self.inflow(src, x, y, turned[2 * n], turned[2 * n + 1])
            fresh = jnp.where(here > 0.0, fresh, 0.0)
            if last:
                total = fresh + pltpu.roll(fresh, 4, 0)
                total = total + pltpu.roll(total, 2, 0)
                total = total + pltpu.roll(total, 1, 0)
                fresh = fresh * (1.0 / jnp.maximum(total, renorm_floor))
            dst[pl.ds(at, SLOTS), :] = fresh

    def product(self, src, cells, turned, sums):
        sums = list(sums)
        for n, (x, y) in enumerate(cells):
            at = aligned(field_row(x, y))
            here = src[pl.ds(at, SLOTS), :]
            inflow = self.inflow(src, x, y, turned[2 * n], turned[2 * n + 1])
            diag = jnp.broadcast_to(self.coef[6, pl.ds(column(x, y), 1), :], (8, LANES))
            image = diag * (here - inflow * (1.0 / step_share))
            for s in range(SLOTS):
                sums[s] = sums[s] + jnp.broadcast_to(src[pl.ds(at + s, 1), :], (8, LANES)) * image
        return tuple(sums)


def run_stage(coef, field_a, field_b, sums, cells_at, steps_of):
    stencil = Stencil(coef)
    fields = (field_a, field_b)
    for level in (1, 2, 3, 4):
        src, dst = fields[(level - 1) % 2], fields[level % 2]
        if level == 4:
            src = field_b
        steps = steps_of(level)

        def one_step(i, sums, level=level, src=src, dst=dst):
            cells = cells_at(level, i)
            turned = stencil.turned(src, cells)
            if level < 4:
                stencil.sweep(src, dst, cells, turned, level == 3)
                return sums
            return stencil.product(src, cells, turned, sums)

        if steps is None:
            sums = one_step(None, sums)
        else:
            start, count, stride = steps
            sums = lax.fori_loop(0, count, lambda n, c, s=start, d=stride, f=one_step: f(s + n * d, c), sums)
    return sums


def inner_kernel(field_in, perm, field_a, field_b, coef, acc):
    del field_in

    def some_coef(n, _):
        fill_coef(perm, coef, [1 + 7 * n + u for u in range(7)])
        return 0

    lax.fori_loop(0, 2, some_coef, 0)

    def cells_at(level, i):
        return [(i + u, y) for u in range(CB // 2 - level) for y in range(level, CB - level)]

    zero = jnp.zeros((8, LANES), F32)
    sums = run_stage(
        coef, field_a, field_b, (zero,) * SLOTS, cells_at, lambda level: (level, 2, CB // 2 - level)
    )
    for s in range(SLOTS):
        acc[8 * s : 8 * s + 8, :] = sums[s]


def strip_kernel(*refs):
    x_a, x_b, y_a, y_b = refs[:4]
    perm, field_a, field_b, coef, acc = refs[9:]

    for even in (True, False):

        @pl.when(is_even("gx") == even)
        def _(even=even):
            high, low = (x_a, x_b) if even else (x_b, x_a)
            for source, start in ((low, -DEPTH), (high, CB)):

                def one_x(x, _, source=source, start=start):
                    for y in range(CB):
                        at = pl.multiple_of((x * CB + y) * SLOTS, 8)
                        field_a[pl.ds(aligned(field_row(start + x, y)), SLOTS), :] = source[pl.ds(at, SLOTS), :]
                    at = pl.multiple_of(SLOTS * FACE + x * CB, 8)
                    perm[pl.ds(column(start + x, 0), CB), :] = source[pl.ds(at, CB), :]
                    return 0

                lax.fori_loop(0, DEPTH, one_x, 0)

        @pl.when(is_even("gy") == even)
        def _(even=even):
            high, low = (y_a, y_b) if even else (y_b, y_a)

            def one_x(x, _):
                for source, start in ((low, -DEPTH), (high, CB)):
                    for y in range(DEPTH):
                        at = pl.multiple_of((x * DEPTH + y) * SLOTS, 8)
                        field_a[pl.ds(aligned(field_row(x, start + y)), SLOTS), :] = source[pl.ds(at, SLOTS), :]
                    perm[pl.ds(column(x, start), DEPTH), :] = source[pl.ds(SLOTS * FACE + x * DEPTH, DEPTH), :]
                return 0

            lax.fori_loop(0, CB, one_x, 0)

    def some_coef(n, _):
        fill_coef(perm, coef, [11 * n + 1 - DEPTH + u for u in range(11)])
        return 0

    lax.fori_loop(0, 2, some_coef, 0)

    def cells_at(level, i):
        across = list(range(level - DEPTH, level)) + list(range(CB - level, CB - level + DEPTH))
        return [c for u in range(CB // 2 - level) for c in [(x, i + u) for x in across] + [(i + u, y) for y in across]]

    sums = tuple(acc[8 * s : 8 * s + 8, :] for s in range(SLOTS))
    sums = run_stage(coef, field_a, field_b, sums, cells_at, lambda level: (level, 2, CB // 2 - level))
    for s in range(SLOTS):
        acc[8 * s : 8 * s + 8, :] = sums[s]


def node_tables():
    node = lax.broadcasted_iota(jnp.int32, (16, LANES), 0)
    lane = lax.broadcasted_iota(jnp.int32, (16, LANES), 1)
    block = lane // CB
    group = jnp.where((node == block) | (node == block + 9), 1.0, 0.0)
    pair = lax.broadcasted_iota(jnp.int32, (128, LANES), 0)
    lane = lax.broadcasted_iota(jnp.int32, (128, LANES), 1)
    one, two = (pair >> 3) & 7, pair & 7
    offset = 13
    for bit, weight in ((2, 9), (1, 3), (0, 1)):
        offset = offset + weight * (((two >> bit) & 1) - ((one >> bit) & 1))
    goes = (lane == 32 * (one >> 1) + offset) & ((one & 1) == (pair >> 6))
    return group, jnp.where(goes, 1.0, 0.0)


def corner_cells(level):
    cells = []
    for x in list(range(level - DEPTH, level)) + list(range(CB - level, CB - level + DEPTH)):
        for y in list(range(level - DEPTH, level)) + list(range(CB - level, CB - level + DEPTH)):
            out_x = max(-x, x - CB + 1, 0)
            out_y = max(-y, y - CB + 1, 0)
            if out_x + out_y <= DEPTH - level:
                cells.append((x, y))
    return cells


def last_kernel(*refs):
    c_a, c_b = refs[:2]
    rows_out, perm, field_a, field_b, coef = refs[7:12]
    acc = refs[6]

    for even in (True, False):

        @pl.when(is_even("gy") == even)
        def _(even=even):
            high, low = (c_a, c_b) if even else (c_b, c_a)
            for source, y_of in ((low, lambda j: -j), (high, lambda j: CB - 1 + j)):
                n = 0
                for x_of in (lambda i: -i, lambda i: CB - 1 + i):
                    for i, j in CORNER:
                        x, y = x_of(i), y_of(j)
                        at = field_row(x, y)
                        field_a[at : at + SLOTS, :] = source[SLOTS * n : SLOTS * n + SLOTS, :]
                        at = SLOTS * 2 * len(CORNER) + n
                        perm[column(x, y) : column(x, y) + 1, :] = source[at : at + 1, :]
                        n += 1

    for x in (-3, -1, CB - 1, CB + 1):
        fill_coef(perm, coef, (x, x + 1))

    sums = tuple(acc[8 * s : 8 * s + 8, :] for s in range(SLOTS))
    sums = run_stage(
        coef, field_a, field_b, sums, lambda level, i: corner_cells(level), lambda level: None
    )
    group, select = node_tables()
    reduced = jnp.concatenate(sums, axis=0)
    dot = functools.partial(
        lax.dot_general, precision=lax.Precision.HIGHEST, preferred_element_type=F32
    )
    per_block = dot(group, reduced, (((1,), (1,)), ((), ())))
    rows_out[...] = dot(per_block[0:8], select[0:64], (((1,), (0,)), ((), ()))) + dot(
        per_block[8:16], select[64:128], (((1,), (0,)), ((), ()))
    )


def basis_kernel(field, out):
    flat = out.reshape(SLOTS * CB * CB, LANES)

    def one_x(x, _):
        for y in range(CB):
            flat[pl.ds(x * CB + y, SLOTS, stride=CB * CB), :] = field[pl.ds(aligned(field_row(x, y)), SLOTS), :]
        return 0

    lax.fori_loop(0, CB, one_x, 0)


def swap_pairs(axis, first):
    count = lax.axis_size(axis)
    pairs = []
    for a in range(first, count - 1, 2):
        pairs += [(a, a + 1), (a + 1, a)]
    return pairs


def swap_both(first, second, axis):
    return (
        lax.ppermute(first, axis, swap_pairs(axis, 0)),
        lax.ppermute(second, axis, swap_pairs(axis, 1)),
    )


def ahead(array, by_x, by_y):
    count_x, count_y = lax.axis_size("gx"), lax.axis_size("gy")
    pairs = [
        (x * count_y + y, (x + by_x) * count_y + y + by_y)
        for x in range(count_x - by_x)
        for y in range(count_y - by_y)
    ]
    return lax.ppermute(array, ("gx", "gy"), pairs)


def params(mib):
    return pltpu.CompilerParams(vmem_limit_bytes=mib * MIB)


def shards(initial_basis, labels, class_perm, support):
    size_x, size_y, size_z = labels.shape
    assert (size_x, size_y, size_z) == (CB, CB, LANES)
    face = in_vmem(FACE_ROWS, LANES)
    field, perm, x_face_a, x_face_b, y_face_a, y_face_b = pl.pallas_call(
        own_kernel,
        out_shape=(in_vmem(*FIELD), in_vmem(*PLAIN), face, face, face, face),
        in_specs=[HBM_SPEC] * 4,
        out_specs=(VMEM_SPEC,) * 6,
        scratch_shapes=[
            pltpu.VMEM((CB // DEPTH, SLOTS, DEPTH, CB, LANES), F32),
            pltpu.VMEM((CB, CB, LANES), jnp.int32),
            pltpu.VMEM((CB, CB, LANES), jnp.int32),
            pltpu.SMEM((NCLASS,), F32),
            pltpu.SemaphoreType.DMA((3 + CB // DEPTH,)),
        ],
        compiler_params=params(4),
        name="own_tile",
    )(*[in_hbm(a) for a in (initial_basis, labels, support, class_perm)])
    x_a, x_b = swap_both(x_face_a, x_face_b, "gx")
    y_a, y_b = swap_both(y_face_a, y_face_b, "gy")
    field_a, field_b, coef, acc = pl.pallas_call(
        inner_kernel,
        out_shape=(in_vmem(*FIELD), in_vmem(*FIELD), in_vmem(*COEF), in_vmem(64, LANES)),
        in_specs=[VMEM_SPEC] * 2,
        out_specs=(VMEM_SPEC,) * 4,
        input_output_aliases={0: 0},
        compiler_params=params(4),
        cost_estimate=pl.CostEstimate(flops=10 * MIB, bytes_accessed=8 * MIB, transcendentals=0),
        name="inner_stage",
    )(pinned(field), pinned(perm))
    corner = in_vmem(CORNER_ROWS, LANES)
    corner_a, corner_b = pl.pallas_call(
        corner_kernel,
        out_shape=(corner, corner),
        in_specs=[VMEM_SPEC] * 3,
        out_specs=(VMEM_SPEC,) * 2,
        compiler_params=params(4),
        name="corners",
    )(pinned(x_a), pinned(x_b), pinned(acc))
    c_a, c_b = swap_both(corner_a, corner_b, "gy")
    perm, field_a, field_b, coef, acc = pl.pallas_call(
        strip_kernel,
        out_shape=(in_vmem(*PLAIN), in_vmem(*FIELD), in_vmem(*FIELD), in_vmem(*COEF), in_vmem(64, LANES)),
        in_specs=[VMEM_SPEC] * 9,
        out_specs=(VMEM_SPEC,) * 5,
        input_output_aliases={4: 0, 5: 1, 6: 2, 7: 3, 8: 4},
        compiler_params=params(4),
        cost_estimate=pl.CostEstimate(flops=10 * MIB, bytes_accessed=8 * MIB, transcendentals=0),
        name="strip_stage",
    )(*[pinned(a) for a in (x_a, x_b, y_a, y_b, perm, field_a, field_b, coef, acc)])
    rows, _, _, field_b, _ = pl.pallas_call(
        last_kernel,
        out_shape=(in_vmem(8, LANES), in_vmem(*PLAIN), in_vmem(*FIELD), in_vmem(*FIELD), in_vmem(*COEF)),
        in_specs=[VMEM_SPEC] * 7,
        out_specs=(VMEM_SPEC,) * 5,
        input_output_aliases={2: 1, 3: 2, 4: 3, 5: 4},
        compiler_params=params(4),
        name="corner_stage",
    )(*[pinned(a) for a in (c_a, c_b, perm, field_a, field_b, coef, acc)])
    from_x = ahead(rows, 1, 0)
    from_y = ahead(rows, 0, 1)
    from_xy = ahead(rows, 1, 1)
    basis = pl.pallas_call(
        basis_kernel,
        out_shape=jax.ShapeDtypeStruct((SLOTS, CB, CB, LANES), F32),
        in_specs=[VMEM_SPEC],
        out_specs=VMEM_SPEC,
        compiler_params=params(4),
        cost_estimate=pl.CostEstimate(flops=0, bytes_accessed=2 * MIB, transcendentals=0),
        name="basis_out",
    )(pinned(field_b))
    coarse = (rows[:, 0:27] + from_x[:, 64:91]) + (from_y[:, 32:59] + from_xy[:, 96:123])
    return basis, coarse.T.reshape(27, 1, 1, LANES // CB)


def solution(mesh):
    return jax.shard_map(
        shards,
        mesh=mesh,
        in_specs=(P(None, "gx", "gy", None), P("gx", "gy", None), P(), P("gx", "gy", None)),
        out_specs=(P(None, "gx", "gy", None), P(None, "gx", "gy", None)),
        check_vma=False,
    )
```

```python
import functools

import jax
import jax.numpy as jnp
from jax import lax
from jax.experimental import pallas as pl
from jax.experimental.pallas import tpu as pltpu
from jax.sharding import PartitionSpec as P

CB = 16
NCLASS = 16
DEPTH = 4
PAD = CB + 2 * DEPTH
CELLS = PAD * PAD
LANES = 128
SLOTS = 8
FACE = DEPTH * CB
CORNER = tuple((i, j) for i in range(1, DEPTH) for j in range(1, DEPTH) if i + j <= DEPTH)
MIB = 1 << 20
FIRST_PAIRS = {"gx": 1, "gy": 0}
F32 = jnp.float32

step_share = 2.0 / 3.0
renorm_floor = 0.5

FIELD = (16 + CELLS * SLOTS, LANES)
PLAIN = (16 + CELLS, LANES)
COEF = (7, 16 + CELLS, LANES)
FACE_ROWS = FACE * (SLOTS + 1)
CORNER_ROWS = 112


def in_vmem(*shape):
    return pltpu.VMEM(shape, F32)


def pinned(array):
    return pltpu.with_memory_space_constraint(array, pltpu.VMEM)


def in_hbm(array):
    return pltpu.with_memory_space_constraint(array, pltpu.HBM)


VMEM_SPEC = pl.BlockSpec(memory_space=pltpu.VMEM)
SMEM_SPEC = pl.BlockSpec(memory_space=pltpu.SMEM)
HBM_SPEC = pl.BlockSpec(memory_space=pltpu.HBM)


def lane_iota():
    return lax.broadcasted_iota(jnp.int32, (8, LANES), 1)


def slot_iota():
    return lax.broadcasted_iota(jnp.int32, (8, LANES), 0)


def aligned(row):
    return row if isinstance(row, int) else pl.multiple_of(row, 8)


def column(x, y):
    return 8 + (x + DEPTH) * PAD + y + DEPTH


def field_row(x, y):
    return 8 + ((x + DEPTH) * PAD + y + DEPTH) * SLOTS


def is_even(axis):
    return lax.rem(lax.axis_index(axis), 2) == FIRST_PAIRS[axis]


def look_up(label, table):
    level = [table[c] for c in range(NCLASS)]
    for bit in range(4):
        chosen = (label & (1 << bit)) != 0
        level = [jnp.where(chosen, high, low) for low, high in zip(level[0::2], level[1::2])]
    return level[0]


def slot_bits():
    keep = jnp.int32(255)
    keep = jnp.where(lax.axis_index("gx") == lax.axis_size("gx") - 1, keep & 0x0F, keep)
    keep = jnp.where(lax.axis_index("gy") == lax.axis_size("gy") - 1, keep & 0x33, keep)
    keep = jnp.where(lane_iota() >= LANES - CB, keep & 0x55, keep)
    return keep & (1 << slot_iota())


def first_weights(basis, start, stride, support_row, bits):
    found = jnp.broadcast_to(support_row, (8, LANES)) & bits
    return jnp.where(found != 0, basis[pl.ds(start, SLOTS, stride=stride), :], 0.0)


def own_kernel(
    basis_hbm, labels_hbm, support_hbm, table_hbm, field, perm, x_a, x_b, y_a, y_b, basis, labels, support, table, sems
):
    fetch_table = pltpu.make_async_copy(table_hbm, table, sems.at[0])
    fetch_labels = pltpu.make_async_copy(labels_hbm, labels, sems.at[1])
    fetch_support = pltpu.make_async_copy(support_hbm, support, sems.at[2])
    fetch_basis = [
        pltpu.make_async_copy(basis_hbm.at[:, pl.ds(DEPTH * part, DEPTH)], basis.at[part], sems.at[3 + part])
        for part in range(CB // DEPTH)
    ]
    for copy in (fetch_table, fetch_labels, fetch_support, *fetch_basis):
        copy.start()
    bits = slot_bits()
    fetch_table.wait()
    fetch_labels.wait()

    def one_perm(x, _):
        for tile in (0, 8):
            perm[pl.ds(column(x, tile), 8), :] = look_up(labels[x, tile : tile + 8, :], table)
        return 0

    lax.fori_loop(0, CB, one_perm, 0, unroll=4)
    fetch_support.wait()
    for copy in fetch_basis:
        copy.wait()
    basis = basis.reshape(SLOTS * CB * CB, LANES)
    support = support.reshape(CB * CB, LANES)

    def one_x(x, _):
        for y in range(CB):
            start = (x // DEPTH) * (SLOTS * FACE) + (x % DEPTH) * CB + y
            field[pl.ds(aligned(field_row(x, y)), SLOTS), :] = first_weights(
                basis, start, FACE, support[pl.ds(x * CB + y, 1), :], bits
            )
        return 0

    lax.fori_loop(0, CB, one_x, 0, unroll=2)

    def x_face(out, start):
        out[SLOTS * FACE : FACE_ROWS, :] = jnp.concatenate(
            [perm[column(start + x, 0) : column(start + x, 0) + CB, :] for x in range(DEPTH)], axis=0
        )
        for x in range(DEPTH):
            rows = CB * SLOTS
            out[x * rows : (x + 1) * rows, :] = field[field_row(start + x, 0) : field_row(start + x, CB), :]

    def y_face(out, start):
        rows = DEPTH * SLOTS
        for x in range(CB):
            at = SLOTS * FACE + x * DEPTH
            out[at : at + DEPTH, :] = perm[column(x, start) : column(x, start + DEPTH), :]
            out[x * rows : (x + 1) * rows, :] = field[field_row(x, start) : field_row(x, start + DEPTH), :]

    for even in (True, False):

        @pl.when(is_even("gx") == even)
        def _(even=even):
            high, low = (x_a, x_b) if even else (x_b, x_a)
            x_face(low, 0)
            x_face(high, CB - DEPTH)

        @pl.when(is_even("gy") == even)
        def _(even=even):
            high, low = (y_a, y_b) if even else (y_b, y_a)
            y_face(low, 0)
            y_face(high, CB - DEPTH)


def corner_kernel(from_a, from_b, inner_done, out_a, out_b):
    del inner_done
    x_even = is_even("gx")
    y_even = is_even("gy")
    for even in (True, False):

        @pl.when(x_even == even)
        def _(even=even):
            high_x, low_x = (from_a, from_b) if even else (from_b, from_a)
            for out, high in ((out_a, y_even), (out_b, jnp.logical_not(y_even))):
                n = 0
                for source, row in ((low_x, lambda i: DEPTH - i), (high_x, lambda i: i - 1)):
                    for i, j in CORNER:
                        cell = row(i) * CB + jnp.where(high, CB - j, j - 1)
                        out[SLOTS * n : SLOTS * n + SLOTS, :] = source[
                            pl.ds(pl.multiple_of(cell * SLOTS, 8), SLOTS), :
                        ]
                        at = SLOTS * 2 * len(CORNER) + n
                        out[at : at + 1, :] = source[pl.ds(SLOTS * FACE + cell, 1), :]
                        n += 1


def conductance(one, two):
    return 2.0 * one * two / jnp.maximum(one + two, 1e-30)


def fill_coef(perm, coef, xs):
    lane = lane_iota()
    for x in xs:
        for tile in range(3):
            at = aligned(column(x, 8 * tile - DEPTH))
            here = perm[pl.ds(at, 8), :]
            x_up = conductance(here, perm[pl.ds(at + PAD, 8), :])
            x_down = conductance(here, perm[pl.ds(at - PAD, 8), :])
            y_up = conductance(here, perm[pl.ds(at + 1, 8), :])
            y_down = conductance(here, perm[pl.ds(at - 1, 8), :])
            z_up = jnp.where(lane == LANES - 1, 0.0, conductance(here, pltpu.roll(here, LANES - 1, 1)))
            z_down = jnp.where(lane == 0, 0.0, conductance(here, pltpu.roll(here, 1, 1)))
            diag = ((x_up + x_down) + (y_up + y_down)) + (z_up + z_down)
            scale = step_share / jnp.maximum(diag, 1e-30)
            for k, term in enumerate((x_up, x_down, y_up, y_down, z_up, z_down)):
                coef[k, pl.ds(at, 8), :] = term * scale
            coef[6, pl.ds(at, 8), :] = diag


class Stencil:
    def __init__(self, coef):
        self.coef = coef
        slot = slot_iota()
        lane = lane_iota()
        self.x_bit = slot >= 4
        self.y_bit = (slot & 2) != 0
        self.z_bit = (slot & 1) != 0
        self.first = (lane % CB) == 0
        self.last = (lane % CB) == CB - 1

    def turned(self, src, cells):
        out = []
        for x, y in cells:
            at = aligned(field_row(x, y))
            here = src[pl.ds(at, SLOTS), :]
            above = jnp.where(self.z_bit, src[pl.ds(at - 1, SLOTS), :], 0.0)
            below = jnp.where(self.z_bit, 0.0, src[pl.ds(at + 1, SLOTS), :])
            out.append(pltpu.roll(jnp.where(self.first, above, here), LANES - 1, 1))
            out.append(pltpu.roll(jnp.where(self.last, below, here), 1, 1))
        return tuple(out)

    def lateral(self, src, x, y):
        at = aligned(field_row(x, y))
        step = PAD * SLOTS

        def read(offset):
            return src[pl.ds(at + offset, SLOTS), :]

        def crosses(place, where):
            return isinstance(place, int) and place in where

        up, down = (-1, CB - 1), (0, CB)
        x_up = jnp.where(self.x_bit, read(step - 4), 0.0) if crosses(x, up) else read(step)
        x_down = jnp.where(self.x_bit, 0.0, read(4 - step)) if crosses(x, down) else read(-step)
        y_up = jnp.where(self.y_bit, read(SLOTS - 2), 0.0) if crosses(y, up) else read(SLOTS)
        y_down = jnp.where(self.y_bit, 0.0, read(2 - SLOTS)) if crosses(y, down) else read(-SLOTS)
        return x_up, x_down, y_up, y_down

    def inflow(self, src, x, y, z_up, z_down):
        at = column(x, y)
        total = None
        for k, value in enumerate((*self.lateral(src, x, y), z_up, z_down)):
            term = jnp.broadcast_to(self.coef[k, pl.ds(at, 1), :], (8, LANES)) * value
            total = term if total is None else total + term
        return total

    def sweep(self, src, dst, cells, turned, last):
        for n, (x, y) in enumerate(cells):
            at = aligned(field_row(x, y))
            here = src[pl.ds(at, SLOTS), :]
            fresh = here * (1.0 - step_share) + self.inflow(src, x, y, turned[2 * n], turned[2 * n + 1])
            fresh = jnp.where(here > 0.0, fresh, 0.0)
            if last:
                total = fresh + pltpu.roll(fresh, 4, 0)
                total = total + pltpu.roll(total, 2, 0)
                total = total + pltpu.roll(total, 1, 0)
                fresh = fresh * (1.0 / jnp.maximum(total, renorm_floor))
            dst[pl.ds(at, SLOTS), :] = fresh

    def product(self, src, cells, turned, sums):
        sums = list(sums)
        for n, (x, y) in enumerate(cells):
            at = aligned(field_row(x, y))
            here = src[pl.ds(at, SLOTS), :]
            inflow = self.inflow(src, x, y, turned[2 * n], turned[2 * n + 1])
            diag = jnp.broadcast_to(self.coef[6, pl.ds(column(x, y), 1), :], (8, LANES))
            image = diag * (here - inflow * (1.0 / step_share))
            for s in range(SLOTS):
                sums[s] = sums[s] + jnp.broadcast_to(src[pl.ds(at + s, 1), :], (8, LANES)) * image
        return tuple(sums)


def run_stage(coef, field_a, field_b, sums, cells_at, steps_of):
    stencil = Stencil(coef)
    fields = (field_a, field_b)
    for level in (1, 2, 3, 4):
        src, dst = fields[(level - 1) % 2], fields[level % 2]
        if level == 4:
            src = field_b
        steps = steps_of(level)

        def one_step(i, sums, level=level, src=src, dst=dst):
            cells = cells_at(level, i)
            turned = stencil.turned(src, cells)
            if level < 4:
                stencil.sweep(src, dst, cells, turned, level == 3)
                return sums
            return stencil.product(src, cells, turned, sums)

        if steps is None:
            sums = one_step(None, sums)
        else:
            start, count, stride = steps
            sums = lax.fori_loop(0, count, lambda n, c, s=start, d=stride, f=one_step: f(s + n * d, c), sums)
    return sums


def inner_kernel(field_in, perm, field_a, field_b, coef, acc):
    del field_in

    def some_coef(n, _):
        fill_coef(perm, coef, [1 + 7 * n + u for u in range(7)])
        return 0

    lax.fori_loop(0, 2, some_coef, 0)

    def cells_at(level, i):
        return [(i + u, y) for u in range(CB // 2 - level) for y in range(level, CB - level)]

    zero = jnp.zeros((8, LANES), F32)
    sums = run_stage(
        coef, field_a, field_b, (zero,) * SLOTS, cells_at, lambda level: (level, 2, CB // 2 - level)
    )
    for s in range(SLOTS):
        acc[8 * s : 8 * s + 8, :] = sums[s]


def strip_kernel(*refs):
    x_a, x_b, y_a, y_b = refs[:4]
    perm, field_a, field_b, coef, acc = refs[9:]

    for even in (True, False):

        @pl.when(is_even("gx") == even)
        def _(even=even):
            high, low = (x_a, x_b) if even else (x_b, x_a)
            for source, start in ((low, -DEPTH), (high, CB)):

                def one_x(x, _, source=source, start=start):
                    for y in range(CB):
                        at = pl.multiple_of((x * CB + y) * SLOTS, 8)
                        field_a[pl.ds(aligned(field_row(start + x, y)), SLOTS), :] = source[pl.ds(at, SLOTS), :]
                    at = pl.multiple_of(SLOTS * FACE + x * CB, 8)
                    perm[pl.ds(column(start + x, 0), CB), :] = source[pl.ds(at, CB), :]
                    return 0

                lax.fori_loop(0, DEPTH, one_x, 0)

        @pl.when(is_even("gy") == even)
        def _(even=even):
            high, low = (y_a, y_b) if even else (y_b, y_a)

            def one_x(x, _):
                for source, start in ((low, -DEPTH), (high, CB)):
                    for y in range(DEPTH):
                        at = pl.multiple_of((x * DEPTH + y) * SLOTS, 8)
                        field_a[pl.ds(aligned(field_row(x, start + y)), SLOTS), :] = source[pl.ds(at, SLOTS), :]
                    perm[pl.ds(column(x, start), DEPTH), :] = source[pl.ds(SLOTS * FACE + x * DEPTH, DEPTH), :]
                return 0

            lax.fori_loop(0, CB, one_x, 0)

    def some_coef(n, _):
        fill_coef(perm, coef, [11 * n + 1 - DEPTH + u for u in range(11)])
        return 0

    lax.fori_loop(0, 2, some_coef, 0)

    def cells_at(level, i):
        across = list(range(level - DEPTH, level)) + list(range(CB - level, CB - level + DEPTH))
        return [c for u in range(CB // 2 - level) for c in [(x, i + u) for x in across] + [(i + u, y) for y in across]]

    sums = tuple(acc[8 * s : 8 * s + 8, :] for s in range(SLOTS))
    sums = run_stage(coef, field_a, field_b, sums, cells_at, lambda level: (level, 2, CB // 2 - level))
    for s in range(SLOTS):
        acc[8 * s : 8 * s + 8, :] = sums[s]


def node_tables():
    node = lax.broadcasted_iota(jnp.int32, (16, LANES), 0)
    lane = lax.broadcasted_iota(jnp.int32, (16, LANES), 1)
    block = lane // CB
    group = jnp.where((node == block) | (node == block + 9), 1.0, 0.0)
    pair = lax.broadcasted_iota(jnp.int32, (128, LANES), 0)
    lane = lax.broadcasted_iota(jnp.int32, (128, LANES), 1)
    one, two = (pair >> 3) & 7, pair & 7
    offset = 13
    for bit, weight in ((2, 9), (1, 3), (0, 1)):
        offset = offset + weight * (((two >> bit) & 1) - ((one >> bit) & 1))
    goes = (lane == 32 * (one >> 1) + offset) & ((one & 1) == (pair >> 6))
    return group, jnp.where(goes, 1.0, 0.0)


def corner_cells(level):
    cells = []
    for x in list(range(level - DEPTH, level)) + list(range(CB - level, CB - level + DEPTH)):
        for y in list(range(level - DEPTH, level)) + list(range(CB - level, CB - level + DEPTH)):
            out_x = max(-x, x - CB + 1, 0)
            out_y = max(-y, y - CB + 1, 0)
            if out_x + out_y <= DEPTH - level:
                cells.append((x, y))
    return cells


def last_kernel(*refs):
    c_a, c_b = refs[:2]
    rows_out, perm, field_a, field_b, coef = refs[7:12]
    acc = refs[6]

    for even in (True, False):

        @pl.when(is_even("gy") == even)
        def _(even=even):
            high, low = (c_a, c_b) if even else (c_b, c_a)
            for source, y_of in ((low, lambda j: -j), (high, lambda j: CB - 1 + j)):
                n = 0
                for x_of in (lambda i: -i, lambda i: CB - 1 + i):
                    for i, j in CORNER:
                        x, y = x_of(i), y_of(j)
                        at = field_row(x, y)
                        field_a[at : at + SLOTS, :] = source[SLOTS * n : SLOTS * n + SLOTS, :]
                        at = SLOTS * 2 * len(CORNER) + n
                        perm[column(x, y) : column(x, y) + 1, :] = source[at : at + 1, :]
                        n += 1

    for x in (-3, -1, CB - 1, CB + 1):
        fill_coef(perm, coef, (x, x + 1))

    sums = tuple(acc[8 * s : 8 * s + 8, :] for s in range(SLOTS))
    sums = run_stage(
        coef, field_a, field_b, sums, lambda level, i: corner_cells(level), lambda level: None
    )
    group, select = node_tables()
    reduced = jnp.concatenate(sums, axis=0)
    dot = functools.partial(
        lax.dot_general, precision=lax.Precision.HIGHEST, preferred_element_type=F32
    )
    per_block = dot(group, reduced, (((1,), (1,)), ((), ())))
    rows_out[...] = dot(per_block[0:8], select[0:64], (((1,), (0,)), ((), ()))) + dot(
        per_block[8:16], select[64:128], (((1,), (0,)), ((), ()))
    )


def basis_kernel(field, out):
    flat = out.reshape(SLOTS * CB * CB, LANES)

    def one_x(x, _):
        for y in range(CB):
            flat[pl.ds(x * CB + y, SLOTS, stride=CB * CB), :] = field[pl.ds(aligned(field_row(x, y)), SLOTS), :]
        return 0

    lax.fori_loop(0, CB, one_x, 0)


def swap_pairs(axis, first):
    count = lax.axis_size(axis)
    pairs = []
    for a in range(first, count - 1, 2):
        pairs += [(a, a + 1), (a + 1, a)]
    return pairs


def swap_both(first, second, axis):
    return (
        lax.ppermute(first, axis, swap_pairs(axis, FIRST_PAIRS[axis])),
        lax.ppermute(second, axis, swap_pairs(axis, 1 - FIRST_PAIRS[axis])),
    )


def ahead(array, by_x, by_y):
    count_x, count_y = lax.axis_size("gx"), lax.axis_size("gy")
    pairs = [
        (x * count_y + y, (x + by_x) * count_y + y + by_y)
        for x in range(count_x - by_x)
        for y in range(count_y - by_y)
    ]
    return lax.ppermute(array, ("gx", "gy"), pairs)


def params(mib):
    return pltpu.CompilerParams(vmem_limit_bytes=mib * MIB)


def shards(initial_basis, labels, class_perm, support):
    size_x, size_y, size_z = labels.shape
    assert (size_x, size_y, size_z) == (CB, CB, LANES)
    face = in_vmem(FACE_ROWS, LANES)
    field, perm, x_face_a, x_face_b, y_face_a, y_face_b = pl.pallas_call(
        own_kernel,
        out_shape=(in_vmem(*FIELD), in_vmem(*PLAIN), face, face, face, face),
        in_specs=[HBM_SPEC] * 4,
        out_specs=(VMEM_SPEC,) * 6,
        scratch_shapes=[
            pltpu.VMEM((CB // DEPTH, SLOTS, DEPTH, CB, LANES), F32),
            pltpu.VMEM((CB, CB, LANES), jnp.int32),
            pltpu.VMEM((CB, CB, LANES), jnp.int32),
            pltpu.SMEM((NCLASS,), F32),
            pltpu.SemaphoreType.DMA((3 + CB // DEPTH,)),
        ],
        compiler_params=params(4),
        name="own_tile",
    )(*[in_hbm(a) for a in (initial_basis, labels, support, class_perm)])
    x_a, x_b = swap_both(x_face_a, x_face_b, "gx")
    y_a, y_b = swap_both(y_face_a, y_face_b, "gy")
    field_a, field_b, coef, acc = pl.pallas_call(
        inner_kernel,
        out_shape=(in_vmem(*FIELD), in_vmem(*FIELD), in_vmem(*COEF), in_vmem(64, LANES)),
        in_specs=[VMEM_SPEC] * 2,
        out_specs=(VMEM_SPEC,) * 4,
        input_output_aliases={0: 0},
        compiler_params=params(4),
        cost_estimate=pl.CostEstimate(flops=10 * MIB, bytes_accessed=8 * MIB, transcendentals=0),
        name="inner_stage",
    )(pinned(field), pinned(perm))
    corner = in_vmem(CORNER_ROWS, LANES)
    corner_a, corner_b = pl.pallas_call(
        corner_kernel,
        out_shape=(corner, corner),
        in_specs=[VMEM_SPEC] * 3,
        out_specs=(VMEM_SPEC,) * 2,
        compiler_params=params(4),
        name="corners",
    )(pinned(x_a), pinned(x_b), pinned(acc))
    c_a, c_b = swap_both(corner_a, corner_b, "gy")
    perm, field_a, field_b, coef, acc = pl.pallas_call(
        strip_kernel,
        out_shape=(in_vmem(*PLAIN), in_vmem(*FIELD), in_vmem(*FIELD), in_vmem(*COEF), in_vmem(64, LANES)),
        in_specs=[VMEM_SPEC] * 9,
        out_specs=(VMEM_SPEC,) * 5,
        input_output_aliases={4: 0, 5: 1, 6: 2, 7: 3, 8: 4},
        compiler_params=params(4),
        cost_estimate=pl.CostEstimate(flops=10 * MIB, bytes_accessed=8 * MIB, transcendentals=0),
        name="strip_stage",
    )(*[pinned(a) for a in (x_a, x_b, y_a, y_b, perm, field_a, field_b, coef, acc)])
    rows, _, _, field_b, _ = pl.pallas_call(
        last_kernel,
        out_shape=(in_vmem(8, LANES), in_vmem(*PLAIN), in_vmem(*FIELD), in_vmem(*FIELD), in_vmem(*COEF)),
        in_specs=[VMEM_SPEC] * 7,
        out_specs=(VMEM_SPEC,) * 5,
        input_output_aliases={2: 1, 3: 2, 4: 3, 5: 4},
        compiler_params=params(4),
        name="corner_stage",
    )(*[pinned(a) for a in (c_a, c_b, perm, field_a, field_b, coef, acc)])
    from_x = ahead(rows, 1, 0)
    from_y = ahead(rows, 0, 1)
    from_xy = ahead(rows, 1, 1)
    basis = pl.pallas_call(
        basis_kernel,
        out_shape=jax.ShapeDtypeStruct((SLOTS, CB, CB, LANES), F32),
        in_specs=[VMEM_SPEC],
        out_specs=VMEM_SPEC,
        compiler_params=params(4),
        cost_estimate=pl.CostEstimate(flops=0, bytes_accessed=2 * MIB, transcendentals=0),
        name="basis_out",
    )(pinned(field_b))
    coarse = (rows[:, 0:27] + from_x[:, 64:91]) + (from_y[:, 32:59] + from_xy[:, 96:123])
    return basis, coarse.T.reshape(27, 1, 1, LANES // CB)


def solution(mesh):
    return jax.shard_map(
        shards,
        mesh=mesh,
        in_specs=(P(None, "gx", "gy", None), P("gx", "gy", None), P(), P("gx", "gy", None)),
        out_specs=(P(None, "gx", "gy", None), P(None, "gx", "gy", None)),
        check_vma=False,
    )
```

```python
import functools

import jax
import jax.numpy as jnp
from jax import lax
from jax.experimental import pallas as pl
from jax.experimental.pallas import tpu as pltpu
from jax.sharding import PartitionSpec as P

CB = 16
NCLASS = 16
DEPTH = 4
PAD = CB + 2 * DEPTH
CELLS = PAD * PAD
LANES = 128
SLOTS = 8
FACE = DEPTH * CB
CORNER = tuple((i, j) for i in range(1, DEPTH) for j in range(1, DEPTH) if i + j <= DEPTH)
MIB = 1 << 20
FIRST_PAIRS = {"gx": 1, "gy": 0}
F32 = jnp.float32

step_share = 2.0 / 3.0
renorm_floor = 0.5

FIELD = (16 + CELLS * SLOTS, LANES)
PLAIN = (16 + CELLS, LANES)
COEF = (7, 16 + CELLS, LANES)
FACE_ROWS = FACE * (SLOTS + 1)
CORNER_ROWS = 112


def in_vmem(*shape):
    return pltpu.VMEM(shape, F32)


def pinned(array):
    return pltpu.with_memory_space_constraint(array, pltpu.VMEM)


def in_hbm(array):
    return pltpu.with_memory_space_constraint(array, pltpu.HBM)


VMEM_SPEC = pl.BlockSpec(memory_space=pltpu.VMEM)
SMEM_SPEC = pl.BlockSpec(memory_space=pltpu.SMEM)
HBM_SPEC = pl.BlockSpec(memory_space=pltpu.HBM)


def lane_iota():
    return lax.broadcasted_iota(jnp.int32, (8, LANES), 1)


def slot_iota():
    return lax.broadcasted_iota(jnp.int32, (8, LANES), 0)


def aligned(row):
    return row if isinstance(row, int) else pl.multiple_of(row, 8)


def column(x, y):
    return 8 + (x + DEPTH) * PAD + y + DEPTH


def field_row(x, y):
    return 8 + ((x + DEPTH) * PAD + y + DEPTH) * SLOTS


def is_even(axis):
    return lax.rem(lax.axis_index(axis), 2) == FIRST_PAIRS[axis]


def look_up(label, table):
    level = [table[c] for c in range(NCLASS)]
    for bit in range(4):
        chosen = (label & (1 << bit)) != 0
        level = [jnp.where(chosen, high, low) for low, high in zip(level[0::2], level[1::2])]
    return level[0]


def slot_bits():
    keep = jnp.int32(255)
    keep = jnp.where(lax.axis_index("gx") == lax.axis_size("gx") - 1, keep & 0x0F, keep)
    keep = jnp.where(lax.axis_index("gy") == lax.axis_size("gy") - 1, keep & 0x33, keep)
    keep = jnp.where(lane_iota() >= LANES - CB, keep & 0x55, keep)
    return keep & (1 << slot_iota())


def first_weights(basis, start, stride, support_row, bits):
    found = jnp.broadcast_to(support_row, (8, LANES)) & bits
    return jnp.where(found != 0, basis[pl.ds(start, SLOTS, stride=stride), :], 0.0)


def own_kernel(
    basis_hbm, labels_hbm, support_hbm, table_hbm, field, perm, x_a, x_b, y_a, y_b, basis, labels, support, table, sems
):
    fetch_table = pltpu.make_async_copy(table_hbm, table, sems.at[0])
    fetch_labels = pltpu.make_async_copy(labels_hbm, labels, sems.at[1])
    fetch_support = pltpu.make_async_copy(support_hbm, support, sems.at[2])
    fetch_basis = [
        pltpu.make_async_copy(basis_hbm.at[:, pl.ds(DEPTH * part, DEPTH)], basis.at[part], sems.at[3 + part])
        for part in range(CB // DEPTH)
    ]
    for copy in (fetch_table, fetch_labels, fetch_support, *fetch_basis):
        copy.start()
    bits = slot_bits()
    fetch_table.wait()
    fetch_labels.wait()

    def one_perm(x, _):
        for tile in (0, 8):
            perm[pl.ds(column(x, tile), 8), :] = look_up(labels[x, tile : tile + 8, :], table)
        return 0

    lax.fori_loop(0, CB, one_perm, 0, unroll=4)
    fetch_support.wait()
    basis = basis.reshape(SLOTS * CB * CB, LANES)
    support = support.reshape(CB * CB, LANES)

    def one_x(x, _):
        for y in range(CB):
            start = (x // DEPTH) * (SLOTS * FACE) + (x % DEPTH) * CB + y
            field[pl.ds(aligned(field_row(x, y)), SLOTS), :] = first_weights(
                basis, start, FACE, support[pl.ds(x * CB + y, 1), :], bits
            )
        return 0

    for part, copy in enumerate(fetch_basis):
        copy.wait()
        lax.fori_loop(DEPTH * part, DEPTH * (part + 1), one_x, 0, unroll=2)

    def x_face(out, start):
        out[SLOTS * FACE : FACE_ROWS, :] = jnp.concatenate(
            [perm[column(start + x, 0) : column(start + x, 0) + CB, :] for x in range(DEPTH)], axis=0
        )
        for x in range(DEPTH):
            rows = CB * SLOTS
            out[x * rows : (x + 1) * rows, :] = field[field_row(start + x, 0) : field_row(start + x, CB), :]

    def y_face(out, start):
        rows = DEPTH * SLOTS
        for x in range(CB):
            at = SLOTS * FACE + x * DEPTH
            out[at : at + DEPTH, :] = perm[column(x, start) : column(x, start + DEPTH), :]
            out[x * rows : (x + 1) * rows, :] = field[field_row(x, start) : field_row(x, start + DEPTH), :]

    for even in (True, False):

        @pl.when(is_even("gx") == even)
        def _(even=even):
            high, low = (x_a, x_b) if even else (x_b, x_a)
            x_face(low, 0)
            x_face(high, CB - DEPTH)

        @pl.when(is_even("gy") == even)
        def _(even=even):
            high, low = (y_a, y_b) if even else (y_b, y_a)
            y_face(low, 0)
            y_face(high, CB - DEPTH)


def corner_kernel(from_a, from_b, inner_done, out_a, out_b):
    del inner_done
    x_even = is_even("gx")
    y_even = is_even("gy")
    for even in (True, False):

        @pl.when(x_even == even)
        def _(even=even):
            high_x, low_x = (from_a, from_b) if even else (from_b, from_a)
            for out, high in ((out_a, y_even), (out_b, jnp.logical_not(y_even))):
                n = 0
                for source, row in ((low_x, lambda i: DEPTH - i), (high_x, lambda i: i - 1)):
                    for i, j in CORNER:
                        cell = row(i) * CB + jnp.where(high, CB - j, j - 1)
                        out[SLOTS * n : SLOTS * n + SLOTS, :] = source[
                            pl.ds(pl.multiple_of(cell * SLOTS, 8), SLOTS), :
                        ]
                        at = SLOTS * 2 * len(CORNER) + n
                        out[at : at + 1, :] = source[pl.ds(SLOTS * FACE + cell, 1), :]
                        n += 1


def conductance(one, two):
    return 2.0 * one * two / jnp.maximum(one + two, 1e-30)


def fill_coef(perm, coef, xs):
    lane = lane_iota()
    for x in xs:
        for tile in range(3):
            at = aligned(column(x, 8 * tile - DEPTH))
            here = perm[pl.ds(at, 8), :]
            x_up = conductance(here, perm[pl.ds(at + PAD, 8), :])
            x_down = conductance(here, perm[pl.ds(at - PAD, 8), :])
            y_up = conductance(here, perm[pl.ds(at + 1, 8), :])
            y_down = conductance(here, perm[pl.ds(at - 1, 8), :])
            z_up = jnp.where(lane == LANES - 1, 0.0, conductance(here, pltpu.roll(here, LANES - 1, 1)))
            z_down = jnp.where(lane == 0, 0.0, conductance(here, pltpu.roll(here, 1, 1)))
            diag = ((x_up + x_down) + (y_up + y_down)) + (z_up + z_down)
            scale = step_share / jnp.maximum(diag, 1e-30)
            for k, term in enumerate((x_up, x_down, y_up, y_down, z_up, z_down)):
                coef[k, pl.ds(at, 8), :] = term * scale
            coef[6, pl.ds(at, 8), :] = diag


class Stencil:
    def __init__(self, coef):
        self.coef = coef
        slot = slot_iota()
        lane = lane_iota()
        self.x_bit = slot >= 4
        self.y_bit = (slot & 2) != 0
        self.z_bit = (slot & 1) != 0
        self.first = (lane % CB) == 0
        self.last = (lane % CB) == CB - 1

    def turned(self, src, cells):
        out = []
        for x, y in cells:
            at = aligned(field_row(x, y))
            here = src[pl.ds(at, SLOTS), :]
            above = jnp.where(self.z_bit, src[pl.ds(at - 1, SLOTS), :], 0.0)
            below = jnp.where(self.z_bit, 0.0, src[pl.ds(at + 1, SLOTS), :])
            out.append(pltpu.roll(jnp.where(self.first, above, here), LANES - 1, 1))
            out.append(pltpu.roll(jnp.where(self.last, below, here), 1, 1))
        return tuple(out)

    def lateral(self, src, x, y):
        at = aligned(field_row(x, y))
        step = PAD * SLOTS

        def read(offset):
            return src[pl.ds(at + offset, SLOTS), :]

        def crosses(place, where):
            return isinstance(place, int) and place in where

        up, down = (-1, CB - 1), (0, CB)
        x_up = jnp.where(self.x_bit, read(step - 4), 0.0) if crosses(x, up) else read(step)
        x_down = jnp.where(self.x_bit, 0.0, read(4 - step)) if crosses(x, down) else read(-step)
        y_up = jnp.where(self.y_bit, read(SLOTS - 2), 0.0) if crosses(y, up) else read(SLOTS)
        y_down = jnp.where(self.y_bit, 0.0, read(2 - SLOTS)) if crosses(y, down) else read(-SLOTS)
        return x_up, x_down, y_up, y_down

    def inflow(self, src, x, y, z_up, z_down):
        at = column(x, y)
        total = None
        for k, value in enumerate((*self.lateral(src, x, y), z_up, z_down)):
            term = jnp.broadcast_to(self.coef[k, pl.ds(at, 1), :], (8, LANES)) * value
            total = term if total is None else total + term
        return total

    def sweep(self, src, dst, cells, turned, last):
        for n, (x, y) in enumerate(cells):
            at = aligned(field_row(x, y))
            here = src[pl.ds(at, SLOTS), :]
            fresh = here * (1.0 - step_share) + self.inflow(src, x, y, turned[2 * n], turned[2 * n + 1])
            fresh = jnp.where(here > 0.0, fresh, 0.0)
            if last:
                total = fresh + pltpu.roll(fresh, 4, 0)
                total = total + pltpu.roll(total, 2, 0)
                total = total + pltpu.roll(total, 1, 0)
                fresh = fresh * (1.0 / jnp.maximum(total, renorm_floor))
            dst[pl.ds(at, SLOTS), :] = fresh

    def product(self, src, cells, turned, sums):
        sums = list(sums)
        for n, (x, y) in enumerate(cells):
            at = aligned(field_row(x, y))
            here = src[pl.ds(at, SLOTS), :]
            inflow = self.inflow(src, x, y, turned[2 * n], turned[2 * n + 1])
            diag = jnp.broadcast_to(self.coef[6, pl.ds(column(x, y), 1), :], (8, LANES))
            image = diag * (here - inflow * (1.0 / step_share))
            for s in range(SLOTS):
                sums[s] = sums[s] + jnp.broadcast_to(src[pl.ds(at + s, 1), :], (8, LANES)) * image
        return tuple(sums)


def run_stage(coef, field_a, field_b, sums, cells_at, steps_of):
    stencil = Stencil(coef)
    fields = (field_a, field_b)
    for level in (1, 2, 3, 4):
        src, dst = fields[(level - 1) % 2], fields[level % 2]
        if level == 4:
            src = field_b
        steps = steps_of(level)

        def one_step(i, sums, level=level, src=src, dst=dst):
            cells = cells_at(level, i)
            turned = stencil.turned(src, cells)
            if level < 4:
                stencil.sweep(src, dst, cells, turned, level == 3)
                return sums
            return stencil.product(src, cells, turned, sums)

        if steps is None:
            sums = one_step(None, sums)
        else:
            start, count, stride = steps
            sums = lax.fori_loop(0, count, lambda n, c, s=start, d=stride, f=one_step: f(s + n * d, c), sums)
    return sums


def inner_kernel(field_in, perm, field_a, field_b, coef, acc):
    del field_in

    def some_coef(n, _):
        fill_coef(perm, coef, [1 + 7 * n + u for u in range(7)])
        return 0

    lax.fori_loop(0, 2, some_coef, 0)

    def cells_at(level, i):
        return [(i + u, y) for u in range(CB - 2 * level) for y in range(level, CB - level)]

    zero = jnp.zeros((8, LANES), F32)
    sums = run_stage(
        coef, field_a, field_b, (zero,) * SLOTS, cells_at, lambda level: (level, 1, CB - 2 * level)
    )
    for s in range(SLOTS):
        acc[8 * s : 8 * s + 8, :] = sums[s]


def strip_kernel(*refs):
    x_a, x_b, y_a, y_b = refs[:4]
    perm, field_a, field_b, coef, acc = refs[9:]

    for even in (True, False):

        @pl.when(is_even("gx") == even)
        def _(even=even):
            high, low = (x_a, x_b) if even else (x_b, x_a)
            for source, start in ((low, -DEPTH), (high, CB)):

                def one_x(x, _, source=source, start=start):
                    for y in range(CB):
                        at = pl.multiple_of((x * CB + y) * SLOTS, 8)
                        field_a[pl.ds(aligned(field_row(start + x, y)), SLOTS), :] = source[pl.ds(at, SLOTS), :]
                    at = pl.multiple_of(SLOTS * FACE + x * CB, 8)
                    perm[pl.ds(column(start + x, 0), CB), :] = source[pl.ds(at, CB), :]
                    return 0

                lax.fori_loop(0, DEPTH, one_x, 0)

        @pl.when(is_even("gy") == even)
        def _(even=even):
            high, low = (y_a, y_b) if even else (y_b, y_a)

            def one_x(x, _):
                for source, start in ((low, -DEPTH), (high, CB)):
                    for y in range(DEPTH):
                        at = pl.multiple_of((x * DEPTH + y) * SLOTS, 8)
                        field_a[pl.ds(aligned(field_row(x, start + y)), SLOTS), :] = source[pl.ds(at, SLOTS), :]
                    perm[pl.ds(column(x, start), DEPTH), :] = source[pl.ds(SLOTS * FACE + x * DEPTH, DEPTH), :]
                return 0

            lax.fori_loop(0, CB, one_x, 0)

    def some_coef(n, _):
        fill_coef(perm, coef, [11 * n + 1 - DEPTH + u for u in range(11)])
        return 0

    lax.fori_loop(0, 2, some_coef, 0)

    def cells_at(level, i):
        across = list(range(level - DEPTH, level)) + list(range(CB - level, CB - level + DEPTH))
        return [c for u in range(CB - 2 * level) for c in [(x, i + u) for x in across] + [(i + u, y) for y in across]]

    sums = tuple(acc[8 * s : 8 * s + 8, :] for s in range(SLOTS))
    sums = run_stage(coef, field_a, field_b, sums, cells_at, lambda level: (level, 1, CB - 2 * level))
    for s in range(SLOTS):
        acc[8 * s : 8 * s + 8, :] = sums[s]


def node_tables():
    node = lax.broadcasted_iota(jnp.int32, (16, LANES), 0)
    lane = lax.broadcasted_iota(jnp.int32, (16, LANES), 1)
    block = lane // CB
    group = jnp.where((node == block) | (node == block + 9), 1.0, 0.0)
    pair = lax.broadcasted_iota(jnp.int32, (128, LANES), 0)
    lane = lax.broadcasted_iota(jnp.int32, (128, LANES), 1)
    one, two = (pair >> 3) & 7, pair & 7
    offset = 13
    for bit, weight in ((2, 9), (1, 3), (0, 1)):
        offset = offset + weight * (((two >> bit) & 1) - ((one >> bit) & 1))
    goes = (lane == 32 * (one >> 1) + offset) & ((one & 1) == (pair >> 6))
    return group, jnp.where(goes, 1.0, 0.0)


def corner_cells(level):
    cells = []
    for x in list(range(level - DEPTH, level)) + list(range(CB - level, CB - level + DEPTH)):
        for y in list(range(level - DEPTH, level)) + list(range(CB - level, CB - level + DEPTH)):
            out_x = max(-x, x - CB + 1, 0)
            out_y = max(-y, y - CB + 1, 0)
            if out_x + out_y <= DEPTH - level:
                cells.append((x, y))
    return cells


def last_kernel(*refs):
    c_a, c_b = refs[:2]
    rows_out, perm, field_a, field_b, coef = refs[7:12]
    acc = refs[6]

    for even in (True, False):

        @pl.when(is_even("gy") == even)
        def _(even=even):
            high, low = (c_a, c_b) if even else (c_b, c_a)
            for source, y_of in ((low, lambda j: -j), (high, lambda j: CB - 1 + j)):
                n = 0
                for x_of in (lambda i: -i, lambda i: CB - 1 + i):
                    for i, j in CORNER:
                        x, y = x_of(i), y_of(j)
                        at = field_row(x, y)
                        field_a[at : at + SLOTS, :] = source[SLOTS * n : SLOTS * n + SLOTS, :]
                        at = SLOTS * 2 * len(CORNER) + n
                        perm[column(x, y) : column(x, y) + 1, :] = source[at : at + 1, :]
                        n += 1

    for x in (-3, -1, CB - 1, CB + 1):
        fill_coef(perm, coef, (x, x + 1))

    sums = tuple(acc[8 * s : 8 * s + 8, :] for s in range(SLOTS))
    sums = run_stage(
        coef, field_a, field_b, sums, lambda level, i: corner_cells(level), lambda level: None
    )
    group, select = node_tables()
    reduced = jnp.concatenate(sums, axis=0)
    dot = functools.partial(
        lax.dot_general, precision=lax.Precision.HIGHEST, preferred_element_type=F32
    )
    per_block = dot(group, reduced, (((1,), (1,)), ((), ())))
    rows_out[...] = dot(per_block[0:8], select[0:64], (((1,), (0,)), ((), ()))) + dot(
        per_block[8:16], select[64:128], (((1,), (0,)), ((), ()))
    )


def basis_kernel(field, out_hbm, out, sems):
    flat = out.reshape(SLOTS * CB * CB, LANES)
    copies = [
        pltpu.make_async_copy(out.at[part], out_hbm.at[:, pl.ds(DEPTH * part, DEPTH)], sems.at[part])
        for part in range(CB // DEPTH)
    ]

    def one_x(x, _):
        for y in range(CB):
            start = (x // DEPTH) * (SLOTS * FACE) + (x % DEPTH) * CB + y
            flat[pl.ds(start, SLOTS, stride=FACE), :] = field[pl.ds(aligned(field_row(x, y)), SLOTS), :]
        return 0

    for part, copy in enumerate(copies):
        lax.fori_loop(DEPTH * part, DEPTH * (part + 1), one_x, 0, unroll=2)
        copy.start()
    for copy in copies:
        copy.wait()


def swap_pairs(axis, first):
    count = lax.axis_size(axis)
    pairs = []
    for a in range(first, count - 1, 2):
        pairs += [(a, a + 1), (a + 1, a)]
    return pairs


def swap_both(first, second, axis):
    return (
        lax.ppermute(first, axis, swap_pairs(axis, FIRST_PAIRS[axis])),
        lax.ppermute(second, axis, swap_pairs(axis, 1 - FIRST_PAIRS[axis])),
    )


def ahead(array, by_x, by_y):
    count_x, count_y = lax.axis_size("gx"), lax.axis_size("gy")
    pairs = [
        (x * count_y + y, (x + by_x) * count_y + y + by_y)
        for x in range(count_x - by_x)
        for y in range(count_y - by_y)
    ]
    return lax.ppermute(array, ("gx", "gy"), pairs)


def params(mib):
    return pltpu.CompilerParams(vmem_limit_bytes=mib * MIB)


def shards(initial_basis, labels, class_perm, support):
    size_x, size_y, size_z = labels.shape
    assert (size_x, size_y, size_z) == (CB, CB, LANES)
    face = in_vmem(FACE_ROWS, LANES)
    field, perm, x_face_a, x_face_b, y_face_a, y_face_b = pl.pallas_call(
        own_kernel,
        out_shape=(in_vmem(*FIELD), in_vmem(*PLAIN), face, face, face, face),
        in_specs=[HBM_SPEC] * 4,
        out_specs=(VMEM_SPEC,) * 6,
        scratch_shapes=[
            pltpu.VMEM((CB // DEPTH, SLOTS, DEPTH, CB, LANES), F32),
            pltpu.VMEM((CB, CB, LANES), jnp.int32),
            pltpu.VMEM((CB, CB, LANES), jnp.int32),
            pltpu.SMEM((NCLASS,), F32),
            pltpu.SemaphoreType.DMA((3 + CB // DEPTH,)),
        ],
        compiler_params=params(4),
        name="own_tile",
    )(*[in_hbm(a) for a in (initial_basis, labels, support, class_perm)])
    x_a, x_b = swap_both(x_face_a, x_face_b, "gx")
    y_a, y_b = swap_both(y_face_a, y_face_b, "gy")
    field_a, field_b, coef, acc = pl.pallas_call(
        inner_kernel,
        out_shape=(in_vmem(*FIELD), in_vmem(*FIELD), in_vmem(*COEF), in_vmem(64, LANES)),
        in_specs=[VMEM_SPEC] * 2,
        out_specs=(VMEM_SPEC,) * 4,
        input_output_aliases={0: 0},
        compiler_params=params(4),
        cost_estimate=pl.CostEstimate(flops=10 * MIB, bytes_accessed=8 * MIB, transcendentals=0),
        name="inner_stage",
    )(pinned(field), pinned(perm))
    corner = in_vmem(CORNER_ROWS, LANES)
    corner_a, corner_b = pl.pallas_call(
        corner_kernel,
        out_shape=(corner, corner),
        in_specs=[VMEM_SPEC] * 3,
        out_specs=(VMEM_SPEC,) * 2,
        compiler_params=params(4),
        name="corners",
    )(pinned(x_a), pinned(x_b), pinned(acc))
    c_a, c_b = swap_both(corner_a, corner_b, "gy")
    perm, field_a, field_b, coef, acc = pl.pallas_call(
        strip_kernel,
        out_shape=(in_vmem(*PLAIN), in_vmem(*FIELD), in_vmem(*FIELD), in_vmem(*COEF), in_vmem(64, LANES)),
        in_specs=[VMEM_SPEC] * 9,
        out_specs=(VMEM_SPEC,) * 5,
        input_output_aliases={4: 0, 5: 1, 6: 2, 7: 3, 8: 4},
        compiler_params=params(4),
        cost_estimate=pl.CostEstimate(flops=10 * MIB, bytes_accessed=8 * MIB, transcendentals=0),
        name="strip_stage",
    )(*[pinned(a) for a in (x_a, x_b, y_a, y_b, perm, field_a, field_b, coef, acc)])
    rows, _, _, field_b, _ = pl.pallas_call(
        last_kernel,
        out_shape=(in_vmem(8, LANES), in_vmem(*PLAIN), in_vmem(*FIELD), in_vmem(*FIELD), in_vmem(*COEF)),
        in_specs=[VMEM_SPEC] * 7,
        out_specs=(VMEM_SPEC,) * 5,
        input_output_aliases={2: 1, 3: 2, 4: 3, 5: 4},
        compiler_params=params(4),
        name="corner_stage",
    )(*[pinned(a) for a in (c_a, c_b, perm, field_a, field_b, coef, acc)])
    from_x = ahead(rows, 1, 0)
    from_y = ahead(rows, 0, 1)
    from_xy = ahead(rows, 1, 1)
    basis = pl.pallas_call(
        basis_kernel,
        out_shape=jax.ShapeDtypeStruct((SLOTS, CB, CB, LANES), F32),
        in_specs=[VMEM_SPEC],
        out_specs=HBM_SPEC,
        scratch_shapes=[
            pltpu.VMEM((CB // DEPTH, SLOTS, DEPTH, CB, LANES), F32),
            pltpu.SemaphoreType.DMA((CB // DEPTH,)),
        ],
        compiler_params=params(4),
        cost_estimate=pl.CostEstimate(flops=0, bytes_accessed=2 * MIB, transcendentals=0),
        name="basis_out",
    )(pinned(field_b))
    coarse = (rows[:, 0:27] + from_x[:, 64:91]) + (from_y[:, 32:59] + from_xy[:, 96:123])
    return basis, coarse.T.reshape(27, 1, 1, LANES // CB)


def solution(mesh):
    return jax.shard_map(
        shards,
        mesh=mesh,
        in_specs=(P(None, "gx", "gy", None), P("gx", "gy", None), P(), P("gx", "gy", None)),
        out_specs=(P(None, "gx", "gy", None), P(None, "gx", "gy", None)),
        check_vma=False,
    )
```

```python
import functools

import jax
import jax.numpy as jnp
from jax import lax
from jax.experimental import pallas as pl
from jax.experimental.pallas import tpu as pltpu
from jax.sharding import PartitionSpec as P

CB = 16
NCLASS = 16
DEPTH = 4
PAD = CB + 2 * DEPTH
CELLS = PAD * PAD
LANES = 128
SLOTS = 8
FACE = DEPTH * CB
CORNER = tuple((i, j) for i in range(1, DEPTH) for j in range(1, DEPTH) if i + j <= DEPTH)
MIB = 1 << 20
FIRST_PAIRS = {"gx": 1, "gy": 0}
F32 = jnp.float32

step_share = 2.0 / 3.0
renorm_floor = 0.5

FIELD = (16 + CELLS * SLOTS, LANES)
PLAIN = (16 + CELLS, LANES)
COEF = (7, 16 + CELLS, LANES)
FACE_ROWS = FACE * (SLOTS + 1)
CORNER_ROWS = 112


def in_vmem(*shape):
    return pltpu.VMEM(shape, F32)


def pinned(array):
    return pltpu.with_memory_space_constraint(array, pltpu.VMEM)


def in_hbm(array):
    return pltpu.with_memory_space_constraint(array, pltpu.HBM)


VMEM_SPEC = pl.BlockSpec(memory_space=pltpu.VMEM)
SMEM_SPEC = pl.BlockSpec(memory_space=pltpu.SMEM)
HBM_SPEC = pl.BlockSpec(memory_space=pltpu.HBM)


def lane_iota():
    return lax.broadcasted_iota(jnp.int32, (8, LANES), 1)


def slot_iota():
    return lax.broadcasted_iota(jnp.int32, (8, LANES), 0)


def aligned(row):
    return row if isinstance(row, int) else pl.multiple_of(row, 8)


def column(x, y):
    return 8 + (x + DEPTH) * PAD + y + DEPTH


def field_row(x, y):
    return 8 + ((x + DEPTH) * PAD + y + DEPTH) * SLOTS


def is_even(axis):
    return lax.rem(lax.axis_index(axis), 2) == FIRST_PAIRS[axis]


def look_up(label, table):
    level = [table[c] for c in range(NCLASS)]
    for bit in range(4):
        chosen = (label & (1 << bit)) != 0
        level = [jnp.where(chosen, high, low) for low, high in zip(level[0::2], level[1::2])]
    return level[0]


def slot_bits():
    keep = jnp.int32(255)
    keep = jnp.where(lax.axis_index("gx") == lax.axis_size("gx") - 1, keep & 0x0F, keep)
    keep = jnp.where(lax.axis_index("gy") == lax.axis_size("gy") - 1, keep & 0x33, keep)
    keep = jnp.where(lane_iota() >= LANES - CB, keep & 0x55, keep)
    return keep & (1 << slot_iota())


def first_weights(basis, start, stride, support_row, bits):
    found = jnp.broadcast_to(support_row, (8, LANES)) & bits
    return jnp.where(found != 0, basis[pl.ds(start, SLOTS, stride=stride), :], 0.0)


def fill_field(field, basis, part, support, bits, x):
    for y in range(CB):
        start = part * (SLOTS * FACE) + (x % DEPTH) * CB + y
        field[pl.ds(aligned(field_row(x, y)), SLOTS), :] = first_weights(
            basis, start, FACE, support[pl.ds(x * CB + y, 1), :], bits
        )


def x_face_kernel(
    basis_hbm, labels_hbm, support_hbm, table_hbm, field, perm, x_a, x_b, middle, support, ends, labels, table, sems
):
    fetch_table = pltpu.make_async_copy(table_hbm, table, sems.at[0])
    fetch_labels = pltpu.make_async_copy(labels_hbm, labels, sems.at[1])
    fetch_support = pltpu.make_async_copy(support_hbm, support, sems.at[2])
    fetch_basis = [
        pltpu.make_async_copy(basis_hbm.at[:, pl.ds(start, DEPTH)], into, sems.at[3 + n])
        for n, (start, into) in enumerate(
            ((0, ends.at[0]), (CB - DEPTH, ends.at[1]), (DEPTH, middle.at[0]), (2 * DEPTH, middle.at[1]))
        )
    ]
    for copy in (fetch_table, fetch_labels, fetch_support, *fetch_basis):
        copy.start()
    bits = slot_bits()
    fetch_table.wait()
    fetch_labels.wait()

    def one_perm(x, _):
        for tile in (0, 8):
            perm[pl.ds(column(x, tile), 8), :] = look_up(labels[x, tile : tile + 8, :], table)
        return 0

    lax.fori_loop(0, CB, one_perm, 0, unroll=4)
    fetch_support.wait()
    flat = ends.reshape(2 * SLOTS * FACE, LANES)
    support = support.reshape(CB * CB, LANES)
    for part, start in enumerate((0, CB - DEPTH)):
        fetch_basis[part].wait()

        def one_x(x, _, part=part):
            fill_field(field, flat, part, support, bits, x)
            return 0

        lax.fori_loop(start, start + DEPTH, one_x, 0, unroll=2)

    def x_face(out, start):
        out[SLOTS * FACE : FACE_ROWS, :] = jnp.concatenate(
            [perm[column(start + x, 0) : column(start + x, 0) + CB, :] for x in range(DEPTH)], axis=0
        )
        for x in range(DEPTH):
            rows = CB * SLOTS
            out[x * rows : (x + 1) * rows, :] = field[field_row(start + x, 0) : field_row(start + x, CB), :]

    for even in (True, False):

        @pl.when(is_even("gx") == even)
        def _(even=even):
            high, low = (x_a, x_b) if even else (x_b, x_a)
            x_face(low, 0)
            x_face(high, CB - DEPTH)

    for copy in fetch_basis[2:]:
        copy.wait()


def y_face_kernel(field_in, perm, middle, support, field, y_a, y_b):
    del field_in
    bits = slot_bits()
    flat = middle.reshape(2 * SLOTS * FACE, LANES)
    support = support.reshape(CB * CB, LANES)
    for part in range(2):

        def one_x(x, _, part=part):
            fill_field(field, flat, part, support, bits, x)
            return 0

        lax.fori_loop(DEPTH * (part + 1), DEPTH * (part + 2), one_x, 0, unroll=2)

    def y_face(out, start):
        rows = DEPTH * SLOTS
        for x in range(CB):
            at = SLOTS * FACE + x * DEPTH
            out[at : at + DEPTH, :] = perm[column(x, start) : column(x, start + DEPTH), :]
            out[x * rows : (x + 1) * rows, :] = field[field_row(x, start) : field_row(x, start + DEPTH), :]

    for even in (True, False):

        @pl.when(is_even("gy") == even)
        def _(even=even):
            high, low = (y_a, y_b) if even else (y_b, y_a)
            y_face(low, 0)
            y_face(high, CB - DEPTH)


def corner_kernel(from_a, from_b, inner_done, out_a, out_b):
    del inner_done
    x_even = is_even("gx")
    y_even = is_even("gy")
    for even in (True, False):

        @pl.when(x_even == even)
        def _(even=even):
            high_x, low_x = (from_a, from_b) if even else (from_b, from_a)
            for out, high in ((out_a, y_even), (out_b, jnp.logical_not(y_even))):
                n = 0
                for source, row in ((low_x, lambda i: DEPTH - i), (high_x, lambda i: i - 1)):
                    for i, j in CORNER:
                        cell = row(i) * CB + jnp.where(high, CB - j, j - 1)
                        out[SLOTS * n : SLOTS * n + SLOTS, :] = source[
                            pl.ds(pl.multiple_of(cell * SLOTS, 8), SLOTS), :
                        ]
                        at = SLOTS * 2 * len(CORNER) + n
                        out[at : at + 1, :] = source[pl.ds(SLOTS * FACE + cell, 1), :]
                        n += 1


def conductance(one, two):
    return 2.0 * one * two / jnp.maximum(one + two, 1e-30)


def fill_coef(perm, coef, xs, tiles=(0, 1, 2)):
    lane = lane_iota()
    for x in xs:
        for tile in tiles:
            at = aligned(column(x, 8 * tile - DEPTH))
            here = perm[pl.ds(at, 8), :]
            x_up = conductance(here, perm[pl.ds(at + PAD, 8), :])
            x_down = conductance(here, perm[pl.ds(at - PAD, 8), :])
            y_up = conductance(here, perm[pl.ds(at + 1, 8), :])
            y_down = conductance(here, perm[pl.ds(at - 1, 8), :])
            z_up = jnp.where(lane == LANES - 1, 0.0, conductance(here, pltpu.roll(here, LANES - 1, 1)))
            z_down = jnp.where(lane == 0, 0.0, conductance(here, pltpu.roll(here, 1, 1)))
            diag = ((x_up + x_down) + (y_up + y_down)) + (z_up + z_down)
            scale = step_share / jnp.maximum(diag, 1e-30)
            for k, term in enumerate((x_up, x_down, y_up, y_down, z_up, z_down)):
                coef[k, pl.ds(at, 8), :] = term * scale
            coef[6, pl.ds(at, 8), :] = diag


class Stencil:
    def __init__(self, coef):
        self.coef = coef
        slot = slot_iota()
        lane = lane_iota()
        self.x_bit = slot >= 4
        self.y_bit = (slot & 2) != 0
        self.z_bit = (slot & 1) != 0
        self.first = (lane % CB) == 0
        self.last = (lane % CB) == CB - 1

    def turned(self, src, cells):
        out = []
        for x, y in cells:
            at = aligned(field_row(x, y))
            here = src[pl.ds(at, SLOTS), :]
            above = jnp.where(self.z_bit, src[pl.ds(at - 1, SLOTS), :], 0.0)
            below = jnp.where(self.z_bit, 0.0, src[pl.ds(at + 1, SLOTS), :])
            out.append(pltpu.roll(jnp.where(self.first, above, here), LANES - 1, 1))
            out.append(pltpu.roll(jnp.where(self.last, below, here), 1, 1))
        return tuple(out)

    def lateral(self, src, x, y):
        at = aligned(field_row(x, y))
        step = PAD * SLOTS

        def read(offset):
            return src[pl.ds(at + offset, SLOTS), :]

        def crosses(place, where):
            return isinstance(place, int) and place in where

        up, down = (-1, CB - 1), (0, CB)
        x_up = jnp.where(self.x_bit, read(step - 4), 0.0) if crosses(x, up) else read(step)
        x_down = jnp.where(self.x_bit, 0.0, read(4 - step)) if crosses(x, down) else read(-step)
        y_up = jnp.where(self.y_bit, read(SLOTS - 2), 0.0) if crosses(y, up) else read(SLOTS)
        y_down = jnp.where(self.y_bit, 0.0, read(2 - SLOTS)) if crosses(y, down) else read(-SLOTS)
        return x_up, x_down, y_up, y_down

    def inflow(self, src, x, y, z_up, z_down):
        at = column(x, y)
        total = None
        for k, value in enumerate((*self.lateral(src, x, y), z_up, z_down)):
            term = jnp.broadcast_to(self.coef[k, pl.ds(at, 1), :], (8, LANES)) * value
            total = term if total is None else total + term
        return total

    def sweep(self, src, dst, cells, turned, last):
        for n, (x, y) in enumerate(cells):
            at = aligned(field_row(x, y))
            here = src[pl.ds(at, SLOTS), :]
            fresh = here * (1.0 - step_share) + self.inflow(src, x, y, turned[2 * n], turned[2 * n + 1])
            fresh = jnp.where(here > 0.0, fresh, 0.0)
            if last:
                total = fresh + pltpu.roll(fresh, 4, 0)
                total = total + pltpu.roll(total, 2, 0)
                total = total + pltpu.roll(total, 1, 0)
                fresh = fresh * (1.0 / jnp.maximum(total, renorm_floor))
            dst[pl.ds(at, SLOTS), :] = fresh

    def product(self, src, cells, turned, sums):
        sums = list(sums)
        for n, (x, y) in enumerate(cells):
            at = aligned(field_row(x, y))
            here = src[pl.ds(at, SLOTS), :]
            inflow = self.inflow(src, x, y, turned[2 * n], turned[2 * n + 1])
            diag = jnp.broadcast_to(self.coef[6, pl.ds(column(x, y), 1), :], (8, LANES))
            image = diag * (here - inflow * (1.0 / step_share))
            for s in range(SLOTS):
                sums[s] = sums[s] + jnp.broadcast_to(src[pl.ds(at + s, 1), :], (8, LANES)) * image
        return tuple(sums)


def run_stage(coef, field_a, field_b, sums, cells_at, steps_of):
    stencil = Stencil(coef)
    fields = (field_a, field_b)
    for level in (1, 2, 3, 4):
        src, dst = fields[(level - 1) % 2], fields[level % 2]
        if level == 4:
            src = field_b
        steps = steps_of(level)

        def one_step(i, sums, level=level, src=src, dst=dst):
            cells = cells_at(level, i)
            turned = stencil.turned(src, cells)
            if level < 4:
                stencil.sweep(src, dst, cells, turned, level == 3)
                return sums
            return stencil.product(src, cells, turned, sums)

        if steps is None:
            sums = one_step(None, sums)
        else:
            start, count, stride = steps
            sums = lax.fori_loop(0, count, lambda n, c, s=start, d=stride, f=one_step: f(s + n * d, c), sums)
    return sums


def inner_kernel(field_in, perm, field_a, field_b, coef, acc):
    del field_in

    def some_coef(n, _):
        fill_coef(perm, coef, [1 + 7 * n + u for u in range(7)])
        return 0

    lax.fori_loop(0, 2, some_coef, 0)

    def cells_at(level, i):
        return [(i + u, y) for u in range(CB - 2 * level) for y in range(level, CB - level)]

    zero = jnp.zeros((8, LANES), F32)
    sums = run_stage(
        coef, field_a, field_b, (zero,) * SLOTS, cells_at, lambda level: (level, 1, CB - 2 * level)
    )
    for s in range(SLOTS):
        acc[8 * s : 8 * s + 8, :] = sums[s]


def strip_kernel(*refs):
    x_a, x_b, y_a, y_b = refs[:4]
    perm, field_a, field_b, coef, acc = refs[9:]

    for even in (True, False):

        @pl.when(is_even("gx") == even)
        def _(even=even):
            high, low = (x_a, x_b) if even else (x_b, x_a)
            for source, start in ((low, -DEPTH), (high, CB)):

                def one_x(x, _, source=source, start=start):
                    for y in range(CB):
                        at = pl.multiple_of((x * CB + y) * SLOTS, 8)
                        field_a[pl.ds(aligned(field_row(start + x, y)), SLOTS), :] = source[pl.ds(at, SLOTS), :]
                    at = pl.multiple_of(SLOTS * FACE + x * CB, 8)
                    perm[pl.ds(column(start + x, 0), CB), :] = source[pl.ds(at, CB), :]
                    return 0

                lax.fori_loop(0, DEPTH, one_x, 0)

        @pl.when(is_even("gy") == even)
        def _(even=even):
            high, low = (y_a, y_b) if even else (y_b, y_a)

            def one_x(x, _):
                for source, start in ((low, -DEPTH), (high, CB)):
                    for y in range(DEPTH):
                        at = pl.multiple_of((x * DEPTH + y) * SLOTS, 8)
                        field_a[pl.ds(aligned(field_row(x, start + y)), SLOTS), :] = source[pl.ds(at, SLOTS), :]
                    perm[pl.ds(column(x, start), DEPTH), :] = source[pl.ds(SLOTS * FACE + x * DEPTH, DEPTH), :]
                return 0

            lax.fori_loop(0, CB, one_x, 0)

    def some_coef(n, _):
        fill_coef(perm, coef, [1 + 7 * n + u for u in range(7)], (0, 2))
        return 0

    fill_coef(perm, coef, [*range(1 - DEPTH, 1), *range(CB - 1, CB + DEPTH - 1)])

    lax.fori_loop(0, 2, some_coef, 0)

    def cells_at(level, i):
        across = list(range(level - DEPTH, level)) + list(range(CB - level, CB - level + DEPTH))
        return [c for u in range(CB - 2 * level) for c in [(x, i + u) for x in across] + [(i + u, y) for y in across]]

    sums = tuple(acc[8 * s : 8 * s + 8, :] for s in range(SLOTS))
    sums = run_stage(coef, field_a, field_b, sums, cells_at, lambda level: (level, 1, CB - 2 * level))
    for s in range(SLOTS):
        acc[8 * s : 8 * s + 8, :] = sums[s]


def node_tables():
    node = lax.broadcasted_iota(jnp.int32, (16, LANES), 0)
    lane = lax.broadcasted_iota(jnp.int32, (16, LANES), 1)
    block = lane // CB
    group = jnp.where((node == block) | (node == block + 9), 1.0, 0.0)
    pair = lax.broadcasted_iota(jnp.int32, (128, LANES), 0)
    lane = lax.broadcasted_iota(jnp.int32, (128, LANES), 1)
    one, two = (pair >> 3) & 7, pair & 7
    offset = 13
    for bit, weight in ((2, 9), (1, 3), (0, 1)):
        offset = offset + weight * (((two >> bit) & 1) - ((one >> bit) & 1))
    goes = (lane == 32 * (one >> 1) + offset) & ((one & 1) == (pair >> 6))
    return group, jnp.where(goes, 1.0, 0.0)


def corner_cells(level):
    cells = []
    for x in list(range(level - DEPTH, level)) + list(range(CB - level, CB - level + DEPTH)):
        for y in list(range(level - DEPTH, level)) + list(range(CB - level, CB - level + DEPTH)):
            out_x = max(-x, x - CB + 1, 0)
            out_y = max(-y, y - CB + 1, 0)
            if out_x + out_y <= DEPTH - level:
                cells.append((x, y))
    return cells


def last_kernel(*refs):
    c_a, c_b = refs[:2]
    rows_out, perm, field_a, field_b, coef = refs[7:12]
    acc = refs[6]

    for even in (True, False):

        @pl.when(is_even("gy") == even)
        def _(even=even):
            high, low = (c_a, c_b) if even else (c_b, c_a)
            for source, y_of in ((low, lambda j: -j), (high, lambda j: CB - 1 + j)):
                n = 0
                for x_of in (lambda i: -i, lambda i: CB - 1 + i):
                    for i, j in CORNER:
                        x, y = x_of(i), y_of(j)
                        at = field_row(x, y)
                        field_a[at : at + SLOTS, :] = source[SLOTS * n : SLOTS * n + SLOTS, :]
                        at = SLOTS * 2 * len(CORNER) + n
                        perm[column(x, y) : column(x, y) + 1, :] = source[at : at + 1, :]
                        n += 1

    for x in (-3, -1, CB - 1, CB + 1):
        fill_coef(perm, coef, (x, x + 1))

    sums = tuple(acc[8 * s : 8 * s + 8, :] for s in range(SLOTS))
    sums = run_stage(
        coef, field_a, field_b, sums, lambda level, i: corner_cells(level), lambda level: None
    )
    group, select = node_tables()
    reduced = jnp.concatenate(sums, axis=0)
    dot = functools.partial(
        lax.dot_general, precision=lax.Precision.HIGHEST, preferred_element_type=F32
    )
    per_block = dot(group, reduced, (((1,), (1,)), ((), ())))
    rows_out[...] = dot(per_block[0:8], select[0:64], (((1,), (0,)), ((), ()))) + dot(
        per_block[8:16], select[64:128], (((1,), (0,)), ((), ()))
    )


def basis_kernel(field, out_hbm, out, sems):
    flat = out.reshape(SLOTS * CB * CB, LANES)
    copies = [
        pltpu.make_async_copy(out.at[part], out_hbm.at[:, pl.ds(DEPTH * part, DEPTH)], sems.at[part])
        for part in range(CB // DEPTH)
    ]

    def one_x(x, _):
        for y in range(CB):
            start = (x // DEPTH) * (SLOTS * FACE) + (x % DEPTH) * CB + y
            flat[pl.ds(start, SLOTS, stride=FACE), :] = field[pl.ds(aligned(field_row(x, y)), SLOTS), :]
        return 0

    for part, copy in enumerate(copies):
        lax.fori_loop(DEPTH * part, DEPTH * (part + 1), one_x, 0, unroll=2)
        copy.start()
    for copy in copies:
        copy.wait()


def swap_pairs(axis, first):
    count = lax.axis_size(axis)
    pairs = []
    for a in range(first, count - 1, 2):
        pairs += [(a, a + 1), (a + 1, a)]
    return pairs


def swap_both(first, second, axis):
    return (
        lax.ppermute(first, axis, swap_pairs(axis, FIRST_PAIRS[axis])),
        lax.ppermute(second, axis, swap_pairs(axis, 1 - FIRST_PAIRS[axis])),
    )


def ahead(array, by_x, by_y):
    count_x, count_y = lax.axis_size("gx"), lax.axis_size("gy")
    pairs = [
        (x * count_y + y, (x + by_x) * count_y + y + by_y)
        for x in range(count_x - by_x)
        for y in range(count_y - by_y)
    ]
    return lax.ppermute(array, ("gx", "gy"), pairs)


def params(mib):
    return pltpu.CompilerParams(vmem_limit_bytes=mib * MIB)


def shards(initial_basis, labels, class_perm, support):
    size_x, size_y, size_z = labels.shape
    assert (size_x, size_y, size_z) == (CB, CB, LANES)
    face = in_vmem(FACE_ROWS, LANES)
    half = (2, SLOTS, DEPTH, CB, LANES)
    bits = pltpu.VMEM((CB, CB, LANES), jnp.int32)
    field, perm, x_face_a, x_face_b, middle, held = pl.pallas_call(
        x_face_kernel,
        out_shape=(in_vmem(*FIELD), in_vmem(*PLAIN), face, face, in_vmem(*half), bits),
        in_specs=[HBM_SPEC] * 4,
        out_specs=(VMEM_SPEC,) * 6,
        scratch_shapes=[
            pltpu.VMEM(half, F32),
            pltpu.VMEM((CB, CB, LANES), jnp.int32),
            pltpu.SMEM((NCLASS,), F32),
            pltpu.SemaphoreType.DMA((7,)),
        ],
        compiler_params=params(4),
        name="x_faces",
    )(*[in_hbm(a) for a in (initial_basis, labels, support, class_perm)])
    x_a, x_b = swap_both(x_face_a, x_face_b, "gx")
    field, y_face_a, y_face_b = pl.pallas_call(
        y_face_kernel,
        out_shape=(in_vmem(*FIELD), face, face),
        in_specs=[VMEM_SPEC] * 4,
        out_specs=(VMEM_SPEC,) * 3,
        input_output_aliases={0: 0},
        compiler_params=params(4),
        name="y_faces",
    )(pinned(field), pinned(perm), pinned(middle), pinned(held))
    y_a, y_b = swap_both(y_face_a, y_face_b, "gy")
    field_a, field_b, coef, acc = pl.pallas_call(
        inner_kernel,
        out_shape=(in_vmem(*FIELD), in_vmem(*FIELD), in_vmem(*COEF), in_vmem(64, LANES)),
        in_specs=[VMEM_SPEC] * 2,
        out_specs=(VMEM_SPEC,) * 4,
        input_output_aliases={0: 0},
        compiler_params=params(4),
        cost_estimate=pl.CostEstimate(flops=10 * MIB, bytes_accessed=8 * MIB, transcendentals=0),
        name="inner_stage",
    )(pinned(field), pinned(perm))
    corner = in_vmem(CORNER_ROWS, LANES)
    corner_a, corner_b = pl.pallas_call(
        corner_kernel,
        out_shape=(corner, corner),
        in_specs=[VMEM_SPEC] * 3,
        out_specs=(VMEM_SPEC,) * 2,
        compiler_params=params(4),
        name="corners",
    )(pinned(x_a), pinned(x_b), pinned(acc))
    c_a, c_b = swap_both(corner_a, corner_b, "gy")
    perm, field_a, field_b, coef, acc = pl.pallas_call(
        strip_kernel,
        out_shape=(in_vmem(*PLAIN), in_vmem(*FIELD), in_vmem(*FIELD), in_vmem(*COEF), in_vmem(64, LANES)),
        in_specs=[VMEM_SPEC] * 9,
        out_specs=(VMEM_SPEC,) * 5,
        input_output_aliases={4: 0, 5: 1, 6: 2, 7: 3, 8: 4},
        compiler_params=params(4),
        cost_estimate=pl.CostEstimate(flops=10 * MIB, bytes_accessed=8 * MIB, transcendentals=0),
        name="strip_stage",
    )(*[pinned(a) for a in (x_a, x_b, y_a, y_b, perm, field_a, field_b, coef, acc)])
    rows, _, _, field_b, _ = pl.pallas_call(
        last_kernel,
        out_shape=(in_vmem(8, LANES), in_vmem(*PLAIN), in_vmem(*FIELD), in_vmem(*FIELD), in_vmem(*COEF)),
        in_specs=[VMEM_SPEC] * 7,
        out_specs=(VMEM_SPEC,) * 5,
        input_output_aliases={2: 1, 3: 2, 4: 3, 5: 4},
        compiler_params=params(4),
        name="corner_stage",
    )(*[pinned(a) for a in (c_a, c_b, perm, field_a, field_b, coef, acc)])
    from_x = ahead(rows, 1, 0)
    from_y = ahead(rows, 0, 1)
    from_xy = ahead(rows, 1, 1)
    basis = pl.pallas_call(
        basis_kernel,
        out_shape=jax.ShapeDtypeStruct((SLOTS, CB, CB, LANES), F32),
        in_specs=[VMEM_SPEC],
        out_specs=HBM_SPEC,
        scratch_shapes=[
            pltpu.VMEM((CB // DEPTH, SLOTS, DEPTH, CB, LANES), F32),
            pltpu.SemaphoreType.DMA((CB // DEPTH,)),
        ],
        compiler_params=params(4),
        cost_estimate=pl.CostEstimate(flops=0, bytes_accessed=2 * MIB, transcendentals=0),
        name="basis_out",
    )(pinned(field_b))
    coarse = (rows[:, 0:27] + from_x[:, 64:91]) + (from_y[:, 32:59] + from_xy[:, 96:123])
    return basis, coarse.T.reshape(27, 1, 1, LANES // CB)


def solution(mesh):
    return jax.shard_map(
        shards,
        mesh=mesh,
        in_specs=(P(None, "gx", "gy", None), P("gx", "gy", None), P(), P("gx", "gy", None)),
        out_specs=(P(None, "gx", "gy", None), P(None, "gx", "gy", None)),
        check_vma=False,
    )
```

```python
import functools

import jax
import jax.numpy as jnp
from jax import lax
from jax.experimental import pallas as pl
from jax.experimental.pallas import tpu as pltpu
from jax.sharding import PartitionSpec as P

CB = 16
NCLASS = 16
DEPTH = 4
PAD = CB + 2 * DEPTH
CELLS = PAD * PAD
LANES = 128
SLOTS = 8
FACE = DEPTH * CB
CORNER = tuple((i, j) for i in range(1, DEPTH) for j in range(1, DEPTH) if i + j <= DEPTH)
MIB = 1 << 20
FIRST_PAIRS = {"gx": 1, "gy": 0}
F32 = jnp.float32

step_share = 2.0 / 3.0
renorm_floor = 0.5

FIELD = (16 + CELLS * SLOTS, LANES)
PLAIN = (16 + CELLS, LANES)
COEF = (7, 16 + CELLS, LANES)
FACE_ROWS = FACE * (SLOTS + 1)
CORNER_ROWS = 112


def in_vmem(*shape):
    return pltpu.VMEM(shape, F32)


def pinned(array):
    return pltpu.with_memory_space_constraint(array, pltpu.VMEM)


def in_hbm(array):
    return pltpu.with_memory_space_constraint(array, pltpu.HBM)


VMEM_SPEC = pl.BlockSpec(memory_space=pltpu.VMEM)
SMEM_SPEC = pl.BlockSpec(memory_space=pltpu.SMEM)
HBM_SPEC = pl.BlockSpec(memory_space=pltpu.HBM)


def lane_iota():
    return lax.broadcasted_iota(jnp.int32, (8, LANES), 1)


def slot_iota():
    return lax.broadcasted_iota(jnp.int32, (8, LANES), 0)


def aligned(row):
    return row if isinstance(row, int) else pl.multiple_of(row, 8)


def column(x, y):
    return 8 + (x + DEPTH) * PAD + y + DEPTH


def field_row(x, y):
    return 8 + ((x + DEPTH) * PAD + y + DEPTH) * SLOTS


def is_even(axis):
    return lax.rem(lax.axis_index(axis), 2) == FIRST_PAIRS[axis]


def look_up(label, table):
    level = [table[c] for c in range(NCLASS)]
    for bit in range(4):
        chosen = (label & (1 << bit)) != 0
        level = [jnp.where(chosen, high, low) for low, high in zip(level[0::2], level[1::2])]
    return level[0]


def slot_bits():
    keep = jnp.int32(255)
    keep = jnp.where(lax.axis_index("gx") == lax.axis_size("gx") - 1, keep & 0x0F, keep)
    keep = jnp.where(lax.axis_index("gy") == lax.axis_size("gy") - 1, keep & 0x33, keep)
    keep = jnp.where(lane_iota() >= LANES - CB, keep & 0x55, keep)
    return keep & (1 << slot_iota())


def first_weights(basis, start, stride, support_row, bits):
    found = jnp.broadcast_to(support_row, (8, LANES)) & bits
    return jnp.where(found != 0, basis[pl.ds(start, SLOTS, stride=stride), :], 0.0)


def fill_field(field, basis, part, support, bits, x):
    for y in range(CB):
        start = part * (SLOTS * FACE) + (x % DEPTH) * CB + y
        field[pl.ds(aligned(field_row(x, y)), SLOTS), :] = first_weights(
            basis, start, FACE, support[pl.ds(x * CB + y, 1), :], bits
        )


def x_face_kernel(
    basis_hbm, labels_hbm, support_hbm, table_hbm, field, perm, x_a, x_b, middle, support, ends, labels, table, sems
):
    fetch_table = pltpu.make_async_copy(table_hbm, table, sems.at[0])
    fetch_labels = pltpu.make_async_copy(labels_hbm, labels, sems.at[1])
    fetch_support = pltpu.make_async_copy(support_hbm, support, sems.at[2])
    fetch_basis = [
        pltpu.make_async_copy(basis_hbm.at[:, pl.ds(start, DEPTH)], into, sems.at[3 + n])
        for n, (start, into) in enumerate(
            ((0, ends.at[0]), (CB - DEPTH, ends.at[1]), (DEPTH, middle.at[0]), (2 * DEPTH, middle.at[1]))
        )
    ]
    for copy in (fetch_table, fetch_labels, fetch_support, *fetch_basis):
        copy.start()
    bits = slot_bits()
    fetch_table.wait()
    fetch_labels.wait()

    def one_perm(x, _):
        for tile in (0, 8):
            perm[pl.ds(column(x, tile), 8), :] = look_up(labels[x, tile : tile + 8, :], table)
        return 0

    lax.fori_loop(0, CB, one_perm, 0, unroll=4)
    fetch_support.wait()
    flat = ends.reshape(2 * SLOTS * FACE, LANES)
    support = support.reshape(CB * CB, LANES)
    for part, start in enumerate((0, CB - DEPTH)):
        fetch_basis[part].wait()

        def one_x(x, _, part=part):
            fill_field(field, flat, part, support, bits, x)
            return 0

        lax.fori_loop(start, start + DEPTH, one_x, 0, unroll=2)

    def x_face(out, start):
        out[SLOTS * FACE : FACE_ROWS, :] = jnp.concatenate(
            [perm[column(start + x, 0) : column(start + x, 0) + CB, :] for x in range(DEPTH)], axis=0
        )
        for x in range(DEPTH):
            rows = CB * SLOTS
            out[x * rows : (x + 1) * rows, :] = field[field_row(start + x, 0) : field_row(start + x, CB), :]

    for even in (True, False):

        @pl.when(is_even("gx") == even)
        def _(even=even):
            high, low = (x_a, x_b) if even else (x_b, x_a)
            x_face(low, 0)
            x_face(high, CB - DEPTH)

    for copy in fetch_basis[2:]:
        copy.wait()


def y_face_kernel(field_in, perm, middle, support, field, y_a, y_b):
    del field_in
    bits = slot_bits()
    flat = middle.reshape(2 * SLOTS * FACE, LANES)
    support = support.reshape(CB * CB, LANES)
    for part in range(2):

        def one_x(x, _, part=part):
            fill_field(field, flat, part, support, bits, x)
            return 0

        lax.fori_loop(DEPTH * (part + 1), DEPTH * (part + 2), one_x, 0, unroll=2)

    def y_face(out, start):
        rows = DEPTH * SLOTS
        for x in range(CB):
            at = SLOTS * FACE + x * DEPTH
            out[at : at + DEPTH, :] = perm[column(x, start) : column(x, start + DEPTH), :]
            out[x * rows : (x + 1) * rows, :] = field[field_row(x, start) : field_row(x, start + DEPTH), :]

    for even in (True, False):

        @pl.when(is_even("gy") == even)
        def _(even=even):
            high, low = (y_a, y_b) if even else (y_b, y_a)
            y_face(low, 0)
            y_face(high, CB - DEPTH)


def corner_kernel(from_a, from_b, inner_done, out_a, out_b):
    del inner_done
    x_even = is_even("gx")
    y_even = is_even("gy")
    for even in (True, False):

        @pl.when(x_even == even)
        def _(even=even):
            high_x, low_x = (from_a, from_b) if even else (from_b, from_a)
            for out, high in ((out_a, y_even), (out_b, jnp.logical_not(y_even))):
                n = 0
                for source, row in ((low_x, lambda i: DEPTH - i), (high_x, lambda i: i - 1)):
                    for i, j in CORNER:
                        cell = row(i) * CB + jnp.where(high, CB - j, j - 1)
                        out[SLOTS * n : SLOTS * n + SLOTS, :] = source[
                            pl.ds(pl.multiple_of(cell * SLOTS, 8), SLOTS), :
                        ]
                        at = SLOTS * 2 * len(CORNER) + n
                        out[at : at + 1, :] = source[pl.ds(SLOTS * FACE + cell, 1), :]
                        n += 1


def conductance(one, two):
    return 2.0 * one * two / jnp.maximum(one + two, 1e-30)


def fill_coef(perm, coef, xs, tiles=(0, 1, 2)):
    lane = lane_iota()
    for x in xs:
        for tile in tiles:
            at = aligned(column(x, 8 * tile - DEPTH))
            here = perm[pl.ds(at, 8), :]
            x_up = conductance(here, perm[pl.ds(at + PAD, 8), :])
            x_down = conductance(here, perm[pl.ds(at - PAD, 8), :])
            y_up = conductance(here, perm[pl.ds(at + 1, 8), :])
            y_down = conductance(here, perm[pl.ds(at - 1, 8), :])
            z_up = jnp.where(lane == LANES - 1, 0.0, conductance(here, pltpu.roll(here, LANES - 1, 1)))
            z_down = jnp.where(lane == 0, 0.0, conductance(here, pltpu.roll(here, 1, 1)))
            diag = ((x_up + x_down) + (y_up + y_down)) + (z_up + z_down)
            scale = step_share / jnp.maximum(diag, 1e-30)
            for k, term in enumerate((x_up, x_down, y_up, y_down, z_up, z_down)):
                coef[k, pl.ds(at, 8), :] = term * scale
            coef[6, pl.ds(at, 8), :] = diag


class Stencil:
    def __init__(self, coef):
        self.coef = coef
        slot = slot_iota()
        lane = lane_iota()
        self.x_bit = slot >= 4
        self.y_bit = (slot & 2) != 0
        self.z_bit = (slot & 1) != 0
        self.first = (lane % CB) == 0
        self.last = (lane % CB) == CB - 1

    def turned(self, src, cells):
        out = []
        for x, y in cells:
            at = aligned(field_row(x, y))
            here = src[pl.ds(at, SLOTS), :]
            above = jnp.where(self.z_bit, src[pl.ds(at - 1, SLOTS), :], 0.0)
            below = jnp.where(self.z_bit, 0.0, src[pl.ds(at + 1, SLOTS), :])
            out.append(pltpu.roll(jnp.where(self.first, above, here), LANES - 1, 1))
            out.append(pltpu.roll(jnp.where(self.last, below, here), 1, 1))
        return tuple(out)

    def lateral(self, src, x, y):
        at = aligned(field_row(x, y))
        step = PAD * SLOTS

        def read(offset):
            return src[pl.ds(at + offset, SLOTS), :]

        def crosses(place, where):
            return isinstance(place, int) and place in where

        up, down = (-1, CB - 1), (0, CB)
        x_up = jnp.where(self.x_bit, read(step - 4), 0.0) if crosses(x, up) else read(step)
        x_down = jnp.where(self.x_bit, 0.0, read(4 - step)) if crosses(x, down) else read(-step)
        y_up = jnp.where(self.y_bit, read(SLOTS - 2), 0.0) if crosses(y, up) else read(SLOTS)
        y_down = jnp.where(self.y_bit, 0.0, read(2 - SLOTS)) if crosses(y, down) else read(-SLOTS)
        return x_up, x_down, y_up, y_down

    def inflow(self, src, x, y, z_up, z_down):
        at = column(x, y)
        total = None
        for k, value in enumerate((*self.lateral(src, x, y), z_up, z_down)):
            term = jnp.broadcast_to(self.coef[k, pl.ds(at, 1), :], (8, LANES)) * value
            total = term if total is None else total + term
        return total

    def sweep(self, src, dst, cells, turned, last):
        for n, (x, y) in enumerate(cells):
            at = aligned(field_row(x, y))
            here = src[pl.ds(at, SLOTS), :]
            fresh = here * (1.0 - step_share) + self.inflow(src, x, y, turned[2 * n], turned[2 * n + 1])
            fresh = jnp.where(here > 0.0, fresh, 0.0)
            if last:
                total = fresh + pltpu.roll(fresh, 4, 0)
                total = total + pltpu.roll(total, 2, 0)
                total = total + pltpu.roll(total, 1, 0)
                fresh = fresh * (1.0 / jnp.maximum(total, renorm_floor))
            dst[pl.ds(at, SLOTS), :] = fresh

    def product(self, src, cells, turned, sums):
        sums = list(sums)
        for n, (x, y) in enumerate(cells):
            at = aligned(field_row(x, y))
            here = src[pl.ds(at, SLOTS), :]
            inflow = self.inflow(src, x, y, turned[2 * n], turned[2 * n + 1])
            diag = jnp.broadcast_to(self.coef[6, pl.ds(column(x, y), 1), :], (8, LANES))
            image = diag * (here - inflow * (1.0 / step_share))
            for s in range(SLOTS):
                sums[s] = sums[s] + jnp.broadcast_to(src[pl.ds(at + s, 1), :], (8, LANES)) * image
        return tuple(sums)


def run_stage(coef, field_a, field_b, sums, cells_at, steps_of):
    stencil = Stencil(coef)
    fields = (field_a, field_b)
    for level in (1, 2, 3, 4):
        src, dst = fields[(level - 1) % 2], fields[level % 2]
        if level == 4:
            src = field_b
        steps = steps_of(level)

        def one_step(i, sums, level=level, src=src, dst=dst):
            cells = cells_at(level, i)
            turned = stencil.turned(src, cells)
            if level < 4:
                stencil.sweep(src, dst, cells, turned, level == 3)
                return sums
            return stencil.product(src, cells, turned, sums)

        if steps is None:
            sums = one_step(None, sums)
        else:
            start, count, stride = steps
            sums = lax.fori_loop(0, count, lambda n, c, s=start, d=stride, f=one_step: f(s + n * d, c), sums)
    return sums


def inner_kernel(field_in, perm, field_a, field_b, coef, acc):
    del field_in

    def some_coef(n, _):
        fill_coef(perm, coef, [1 + 7 * n + u for u in range(7)])
        return 0

    lax.fori_loop(0, 2, some_coef, 0)

    def cells_at(level, i):
        return [(i + u, y) for u in range(CB - 2 * level) for y in range(level, CB - level)]

    zero = jnp.zeros((8, LANES), F32)
    sums = run_stage(
        coef, field_a, field_b, (zero,) * SLOTS, cells_at, lambda level: (level, 1, CB - 2 * level)
    )
    for s in range(SLOTS):
        acc[8 * s : 8 * s + 8, :] = sums[s]


def strip_stage(coef, field_a, field_b, acc, cells_of):
    def cells_at(level, i):
        across = list(range(level - DEPTH, level)) + list(range(CB - level, CB - level + DEPTH))
        return [c for u in range(CB - 2 * level) for c in cells_of(across, i + u)]

    sums = tuple(acc[8 * s : 8 * s + 8, :] for s in range(SLOTS))
    sums = run_stage(coef, field_a, field_b, sums, cells_at, lambda level: (level, 1, CB - 2 * level))
    for s in range(SLOTS):
        acc[8 * s : 8 * s + 8, :] = sums[s]


def x_strip_kernel(*refs):
    x_a, x_b = refs[:2]
    perm, field_a, field_b, coef, acc = refs[7:]

    for even in (True, False):

        @pl.when(is_even("gx") == even)
        def _(even=even):
            high, low = (x_a, x_b) if even else (x_b, x_a)
            for source, start in ((low, -DEPTH), (high, CB)):

                def one_x(x, _, source=source, start=start):
                    for y in range(CB):
                        at = pl.multiple_of((x * CB + y) * SLOTS, 8)
                        field_a[pl.ds(aligned(field_row(start + x, y)), SLOTS), :] = source[pl.ds(at, SLOTS), :]
                    at = pl.multiple_of(SLOTS * FACE + x * CB, 8)
                    perm[pl.ds(column(start + x, 0), CB), :] = source[pl.ds(at, CB), :]
                    return 0

                lax.fori_loop(0, DEPTH, one_x, 0)

    fill_coef(perm, coef, [*range(1 - DEPTH, 1), *range(CB - 1, CB + DEPTH - 1)])
    strip_stage(coef, field_a, field_b, acc, lambda across, i: [(x, i) for x in across])


def y_strip_kernel(*refs):
    y_a, y_b = refs[:2]
    perm, field_a, field_b, coef, acc = refs[7:]

    for even in (True, False):

        @pl.when(is_even("gy") == even)
        def _(even=even):
            high, low = (y_a, y_b) if even else (y_b, y_a)

            def one_x(x, _):
                for source, start in ((low, -DEPTH), (high, CB)):
                    for y in range(DEPTH):
                        at = pl.multiple_of((x * DEPTH + y) * SLOTS, 8)
                        field_a[pl.ds(aligned(field_row(x, start + y)), SLOTS), :] = source[pl.ds(at, SLOTS), :]
                    perm[pl.ds(column(x, start), DEPTH), :] = source[pl.ds(SLOTS * FACE + x * DEPTH, DEPTH), :]
                return 0

            lax.fori_loop(0, CB, one_x, 0)

    def some_coef(n, _):
        fill_coef(perm, coef, [1 + 7 * n + u for u in range(7)], (0, 2))
        return 0

    lax.fori_loop(0, 2, some_coef, 0)
    strip_stage(coef, field_a, field_b, acc, lambda across, i: [(i, y) for y in across])


def node_tables():
    node = lax.broadcasted_iota(jnp.int32, (16, LANES), 0)
    lane = lax.broadcasted_iota(jnp.int32, (16, LANES), 1)
    block = lane // CB
    group = jnp.where((node == block) | (node == block + 9), 1.0, 0.0)
    pair = lax.broadcasted_iota(jnp.int32, (128, LANES), 0)
    lane = lax.broadcasted_iota(jnp.int32, (128, LANES), 1)
    one, two = (pair >> 3) & 7, pair & 7
    offset = 13
    for bit, weight in ((2, 9), (1, 3), (0, 1)):
        offset = offset + weight * (((two >> bit) & 1) - ((one >> bit) & 1))
    goes = (lane == 32 * (one >> 1) + offset) & ((one & 1) == (pair >> 6))
    return group, jnp.where(goes, 1.0, 0.0)


def corner_cells(level):
    cells = []
    for x in list(range(level - DEPTH, level)) + list(range(CB - level, CB - level + DEPTH)):
        for y in list(range(level - DEPTH, level)) + list(range(CB - level, CB - level + DEPTH)):
            out_x = max(-x, x - CB + 1, 0)
            out_y = max(-y, y - CB + 1, 0)
            if out_x + out_y <= DEPTH - level:
                cells.append((x, y))
    return cells


def last_kernel(*refs):
    c_a, c_b = refs[:2]
    rows_out, perm, field_a, field_b, coef = refs[7:12]
    acc = refs[6]

    for even in (True, False):

        @pl.when(is_even("gy") == even)
        def _(even=even):
            high, low = (c_a, c_b) if even else (c_b, c_a)
            for source, y_of in ((low, lambda j: -j), (high, lambda j: CB - 1 + j)):
                n = 0
                for x_of in (lambda i: -i, lambda i: CB - 1 + i):
                    for i, j in CORNER:
                        x, y = x_of(i), y_of(j)
                        at = field_row(x, y)
                        field_a[at : at + SLOTS, :] = source[SLOTS * n : SLOTS * n + SLOTS, :]
                        at = SLOTS * 2 * len(CORNER) + n
                        perm[column(x, y) : column(x, y) + 1, :] = source[at : at + 1, :]
                        n += 1

    for x in (-3, -1, CB - 1, CB + 1):
        fill_coef(perm, coef, (x, x + 1))

    sums = tuple(acc[8 * s : 8 * s + 8, :] for s in range(SLOTS))
    sums = run_stage(
        coef, field_a, field_b, sums, lambda level, i: corner_cells(level), lambda level: None
    )
    group, select = node_tables()
    reduced = jnp.concatenate(sums, axis=0)
    dot = functools.partial(
        lax.dot_general, precision=lax.Precision.HIGHEST, preferred_element_type=F32
    )
    per_block = dot(group, reduced, (((1,), (1,)), ((), ())))
    rows_out[...] = dot(per_block[0:8], select[0:64], (((1,), (0,)), ((), ()))) + dot(
        per_block[8:16], select[64:128], (((1,), (0,)), ((), ()))
    )


def basis_kernel(field, out_hbm, out, sems):
    flat = out.reshape(SLOTS * CB * CB, LANES)
    copies = [
        pltpu.make_async_copy(out.at[part], out_hbm.at[:, pl.ds(DEPTH * part, DEPTH)], sems.at[part])
        for part in range(CB // DEPTH)
    ]

    def one_x(x, _):
        for y in range(CB):
            start = (x // DEPTH) * (SLOTS * FACE) + (x % DEPTH) * CB + y
            flat[pl.ds(start, SLOTS, stride=FACE), :] = field[pl.ds(aligned(field_row(x, y)), SLOTS), :]
        return 0

    for part, copy in enumerate(copies):
        lax.fori_loop(DEPTH * part, DEPTH * (part + 1), one_x, 0, unroll=2)
        copy.start()
    for copy in copies:
        copy.wait()


def swap_pairs(axis, first):
    count = lax.axis_size(axis)
    pairs = []
    for a in range(first, count - 1, 2):
        pairs += [(a, a + 1), (a + 1, a)]
    return pairs


def swap_both(first, second, axis):
    return (
        lax.ppermute(first, axis, swap_pairs(axis, FIRST_PAIRS[axis])),
        lax.ppermute(second, axis, swap_pairs(axis, 1 - FIRST_PAIRS[axis])),
    )


def ahead(array, by_x, by_y):
    count_x, count_y = lax.axis_size("gx"), lax.axis_size("gy")
    pairs = [
        (x * count_y + y, (x + by_x) * count_y + y + by_y)
        for x in range(count_x - by_x)
        for y in range(count_y - by_y)
    ]
    return lax.ppermute(array, ("gx", "gy"), pairs)


def params(mib):
    return pltpu.CompilerParams(vmem_limit_bytes=mib * MIB)


def shards(initial_basis, labels, class_perm, support):
    size_x, size_y, size_z = labels.shape
    assert (size_x, size_y, size_z) == (CB, CB, LANES)
    face = in_vmem(FACE_ROWS, LANES)
    half = (2, SLOTS, DEPTH, CB, LANES)
    bits = pltpu.VMEM((CB, CB, LANES), jnp.int32)
    field, perm, x_face_a, x_face_b, middle, held = pl.pallas_call(
        x_face_kernel,
        out_shape=(in_vmem(*FIELD), in_vmem(*PLAIN), face, face, in_vmem(*half), bits),
        in_specs=[HBM_SPEC] * 4,
        out_specs=(VMEM_SPEC,) * 6,
        scratch_shapes=[
            pltpu.VMEM(half, F32),
            pltpu.VMEM((CB, CB, LANES), jnp.int32),
            pltpu.SMEM((NCLASS,), F32),
            pltpu.SemaphoreType.DMA((7,)),
        ],
        compiler_params=params(4),
        name="x_faces",
    )(*[in_hbm(a) for a in (initial_basis, labels, support, class_perm)])
    x_a, x_b = swap_both(x_face_a, x_face_b, "gx")
    field, y_face_a, y_face_b = pl.pallas_call(
        y_face_kernel,
        out_shape=(in_vmem(*FIELD), face, face),
        in_specs=[VMEM_SPEC] * 4,
        out_specs=(VMEM_SPEC,) * 3,
        input_output_aliases={0: 0},
        compiler_params=params(4),
        name="y_faces",
    )(pinned(field), pinned(perm), pinned(middle), pinned(held))
    y_a, y_b = swap_both(y_face_a, y_face_b, "gy")
    field_a, field_b, coef, acc = pl.pallas_call(
        inner_kernel,
        out_shape=(in_vmem(*FIELD), in_vmem(*FIELD), in_vmem(*COEF), in_vmem(64, LANES)),
        in_specs=[VMEM_SPEC] * 2,
        out_specs=(VMEM_SPEC,) * 4,
        input_output_aliases={0: 0},
        compiler_params=params(4),
        cost_estimate=pl.CostEstimate(flops=10 * MIB, bytes_accessed=8 * MIB, transcendentals=0),
        name="inner_stage",
    )(pinned(field), pinned(perm))
    corner = in_vmem(CORNER_ROWS, LANES)
    corner_a, corner_b = pl.pallas_call(
        corner_kernel,
        out_shape=(corner, corner),
        in_specs=[VMEM_SPEC] * 3,
        out_specs=(VMEM_SPEC,) * 2,
        compiler_params=params(4),
        name="corners",
    )(pinned(x_a), pinned(x_b), pinned(acc))
    c_a, c_b = swap_both(corner_a, corner_b, "gy")
    state = (perm, field_a, field_b, coef, acc)
    for kernel, halos in ((x_strip_kernel, (x_a, x_b)), (y_strip_kernel, (y_a, y_b))):
        state = pl.pallas_call(
            kernel,
            out_shape=(in_vmem(*PLAIN), in_vmem(*FIELD), in_vmem(*FIELD), in_vmem(*COEF), in_vmem(64, LANES)),
            in_specs=[VMEM_SPEC] * 7,
            out_specs=(VMEM_SPEC,) * 5,
            input_output_aliases={2 + n: n for n in range(5)},
            compiler_params=params(4),
            cost_estimate=pl.CostEstimate(flops=10 * MIB, bytes_accessed=8 * MIB, transcendentals=0),
            name=kernel.__name__,
        )(*[pinned(a) for a in (*halos, *state)])
    rows, _, _, field_b, _ = pl.pallas_call(
        last_kernel,
        out_shape=(in_vmem(8, LANES), in_vmem(*PLAIN), in_vmem(*FIELD), in_vmem(*FIELD), in_vmem(*COEF)),
        in_specs=[VMEM_SPEC] * 7,
        out_specs=(VMEM_SPEC,) * 5,
        input_output_aliases={2: 1, 3: 2, 4: 3, 5: 4},
        compiler_params=params(4),
        name="corner_stage",
    )(*[pinned(a) for a in (c_a, c_b, *state)])
    from_x = ahead(rows, 1, 0)
    from_y = ahead(rows, 0, 1)
    from_xy = ahead(rows, 1, 1)
    basis = pl.pallas_call(
        basis_kernel,
        out_shape=jax.ShapeDtypeStruct((SLOTS, CB, CB, LANES), F32),
        in_specs=[VMEM_SPEC],
        out_specs=HBM_SPEC,
        scratch_shapes=[
            pltpu.VMEM((CB // DEPTH, SLOTS, DEPTH, CB, LANES), F32),
            pltpu.SemaphoreType.DMA((CB // DEPTH,)),
        ],
        compiler_params=params(4),
        cost_estimate=pl.CostEstimate(flops=0, bytes_accessed=2 * MIB, transcendentals=0),
        name="basis_out",
    )(pinned(field_b))
    coarse = (rows[:, 0:27] + from_x[:, 64:91]) + (from_y[:, 32:59] + from_xy[:, 96:123])
    return basis, coarse.T.reshape(27, 1, 1, LANES // CB)


def solution(mesh):
    return jax.shard_map(
        shards,
        mesh=mesh,
        in_specs=(P(None, "gx", "gy", None), P("gx", "gy", None), P(), P("gx", "gy", None)),
        out_specs=(P(None, "gx", "gy", None), P(None, "gx", "gy", None)),
        check_vma=False,
    )
```
